512 devices in a mesh: les: 128 (over z, x, y_hi), cnn: 4 (over y_lo, core).
Axes of the slice: x: 4, y: 4 (y_hi: 2, y_lo: 2; y = y_hi * 2 + y_lo), z: 16, core: 2. Of those that a mesh axis runs over, the one named last changes fastest.
Arguments:
- velocity: float32 [3, 256, 256, 512], P(None, 'les', None, 'cnn'), may hold values from -6 to 6
- target_stress: bfloat16 [2, 256, 512, 2], P(None, 'les', 'cnn'), may hold values from -6 to 6
- owner_map: int32 [32768, 1], P(('les', 'cnn')), may hold values from 0 to 127; in each aligned block of 64 rows (0 to 63, 64 to 127, ...) at most 2 rows name the same one
- train_order: int32 [512, 64], P(('les', 'cnn')), may hold values from 0 to 63, each once within a row
- w_first: bfloat16 [128, 432, 128], P('les'), may hold values from -0.3125 to 0.3125
- w_mid: bfloat16 [128, 1152, 128], P('les'), may hold values from -0.1875 to 0.1875
- w_out: bfloat16 [128, 128, 2], P('les'), may hold values from -0.5 to 0.5
Outputs:
- new_velocity: float32 [3, 256, 256, 512], P(None, 'les', None, 'cnn')
- wall_stress: float32 [2, 256, 512, 2], P(None, 'les', 'cnn')
- grad_first: float32 [128, 432, 128], P('les')
- grad_mid: float32 [128, 1152, 128], P('les')
- grad_out: float32 [128, 128, 2], P('les')
The draws below stay inside these ranges and needn't reach their ends.
Inputs may be any that keep to these rules, and one draw needn't show every extreme that they name: `owner_map`: among the tiles of one device at most 2 name the same expert, a bound that some block reaches of them. `train_order`: each row holds every rank once.
All inputs are finite; a program needn't handle non-finite values.
Results may differ from the reference program's by a relative error of at most 0.005.
Values may be sent and summed in bfloat16 or wider, within the bound.
A program may use at most 64 MiB of HBM per device.

```python
import math
import jax
import jax.numpy as jnp
import numpy as np
from jax import lax

CX = 128
CZ = 2
NY = 256
TX = 4
NPL = 16
C = 128
CIN = 48
TILE_DEV = 64
CAP = 2
EXPERTS = 128
NZ = 256
NX = 512
TILES = 32768
N_LES = 128
N_CNN = 4


def block_levels(own_key, extent, cuts, smallest, high):
    level, own = 1.0, jax.random.fold_in(own_key, 6)
    for position, shards_of in cuts:
        heights = jnp.exp(jax.random.uniform(jax.random.fold_in(own, position), (shards_of,), jnp.float32, smallest / len(cuts), high / len(cuts)))
        level = level * jnp.repeat(heights, extent[position] // shards_of).reshape([-1 if axis == position else 1 for axis in range(len(extent))])
    return level


def routed_block(key, own, number, rows, amount, top, limit, lean):
    order = jax.random.permutation(key, amount)
    packed, common = portions_of(amount, rows * top, limit, lean, True), portions_of(amount, rows * top, limit, lean, False)
    places = jnp.arange(amount)

    def named(lengths, rotation):
        used = int((lengths > 0).sum())
        fixed = max(1, used // 4)
        moved = fixed + (places - fixed + rotation * (used - fixed)) % max(1, amount - fixed)
        return jnp.zeros((amount,), jnp.int32).at[order[jnp.where(places < fixed, places, moved)]].set(jnp.asarray(lengths, jnp.int32))

    lengths = jnp.where(number % 4 == 0, named(packed, number // 4), named(common, number - number // 4 - 1))
    mixed = jax.random.permutation(jax.random.fold_in(own, 3), amount)
    giver, sink = mixed[0:amount // 2 * 2:2], mixed[1:amount // 2 * 2:2]
    slack = jnp.minimum(lengths[giver] - 1, limit - lengths[sink]) // 2
    slack = jnp.where((giver == order[0]) | (sink == order[0]) | (lengths[sink] == 0), 0, jnp.maximum(slack, 0))
    moved = jax.random.randint(jax.random.fold_in(own, 4), (amount // 2,), 0, 1 << 20) % (slack + 1)
    lengths = lengths.at[giver].add(-moved).at[sink].add(moved)
    members = jnp.searchsorted(jnp.cumsum(lengths), jnp.arange(rows * top), side="right").astype(jnp.int32)
    table = members.reshape(top, rows).T
    table = table[jax.random.permutation(jax.random.fold_in(own, 1), rows)]
    rotation = jax.random.randint(jax.random.fold_in(own, 2), (rows, 1), 0, top)
    return jnp.take_along_axis(table, (jnp.arange(top)[None, :] + rotation) % top, axis=1)


def portions_of(count, total, bound, lean, full):
    portions = [(1 << 20) // math.isqrt(rank ** lean) + 1 for rank in range(1, count + 1)]
    largest = bound if full else min(bound, max(-(-total // count), total * portions[0] // sum(portions)))
    least = 1 if total - largest >= count - 1 else 0
    holding, rest = [largest] + [least] * (count - 1), total - largest - least * (count - 1)
    while rest > 0:
        candidates = [i for i in range(1, count) if holding[i] < largest] or [i for i in range(1, count) if holding[i] < bound]
        pool, budget = sum([portions[i] for i in candidates]), rest
        for i in candidates:
            more = min(bound - holding[i], max(1, budget * portions[i] // pool), rest)
            holding[i] = holding[i] + more
            rest = rest - more
    return np.array(holding)


def scatter_about(own_key, dims, scale, bound, split=(), kind=jnp.bfloat16):
    factor_of = block_levels(own_key, dims, split, -0.22, 0.18) if split else 1.0
    values = jax.random.normal(own_key, dims, jnp.float32) * scale * factor_of
    return jnp.minimum(jnp.maximum(values, -bound), bound).astype(kind)


def setup_inputs(seed: int = 0) -> dict:
    key_list = jax.random.split(jax.random.key(seed), 8)
    velocity = scatter_about(key_list[0], (3, NZ, NY, NX), 1.0, 6.0, ((1, 128), (3, 4)), jnp.float32)
    target_stress = scatter_about(key_list[1], (2, NZ, NX, 2), 1.0, 6.0, ((1, 128), (2, 4)))
    owner_map_keys = jax.random.split(jax.random.fold_in(key_list[2], 1), TILES // TILE_DEV)
    owner_map_turns = jax.random.permutation(jax.random.fold_in(key_list[2], 3), TILES // TILE_DEV)
    owner_map = jax.vmap(lambda own, number: routed_block(jax.random.fold_in(key_list[2], 2), own, number, TILE_DEV, N_LES, 1, CAP, 2))(owner_map_keys, owner_map_turns).reshape((TILES, 1))
    train_order = jax.vmap(lambda own: jax.random.permutation(own, TILE_DEV))(jax.random.split(key_list[3], (N_LES * N_CNN))).reshape((N_LES * N_CNN, TILE_DEV)).astype(jnp.int32)
    w_first = scatter_about(key_list[4], (EXPERTS, 9 * CIN, C), (9 * CIN) ** -0.5, 0.3125, ((0, 128),))
    w_mid = scatter_about(key_list[5], (EXPERTS, 9 * C, C), (9 * C) ** -0.5, 0.1875, ((0, 128),))
    w_out = scatter_about(key_list[6], (EXPERTS, C, 2), C ** -0.5, 0.5, ((0, 128),))
    return dict(velocity=velocity, target_stress=target_stress, owner_map=owner_map, train_order=train_order, w_first=w_first, w_mid=w_mid, w_out=w_out)


DT_STEP = 0.25
VISCOSITY = 0.05
FORCING = 0.2

def patches(values, mirror):
    height = values.shape[1]
    breadth = values.shape[2]
    padded = jnp.pad(values, ((0, 0), (1, 1), (1, 1), (0, 0)))
    pieces = []
    for shift_z in (-1, 0, 1):
        for shift_x in (-1, 0, 1):
            start_z = 1 + mirror * shift_z
            start_x = 1 + mirror * shift_x
            pieces.append(padded[:, start_z:start_z + height, start_x:start_x + breadth, :])
    return jnp.concatenate(pieces, axis=3)

def silu_slope(values):
    logistic = jax.nn.sigmoid(values)
    return logistic * (1.0 + values * (1.0 - logistic))

def tendency(padded):
    center = padded[:, 1:-1, :, 1:-1]
    mirror = jnp.array([1.0, -1.0, 1.0], dtype=center.dtype)[:, None, None, None]
    column = jnp.concatenate([center[:, :, :1, :] * mirror, center, center[:, :, -1:, :] * mirror], axis=2)
    x_plus = padded[:, 1:-1, :, 2:]
    x_minus = padded[:, 1:-1, :, :-2]
    z_plus = padded[:, 2:, :, 1:-1]
    z_minus = padded[:, :-2, :, 1:-1]
    y_plus = column[:, :, 2:, :]
    y_minus = column[:, :, :-2, :]
    advect = 0.5 * (center[0:1] * (x_plus - x_minus) + center[1:2] * (y_plus - y_minus) + center[2:3] * (z_plus - z_minus))
    laplace = x_plus + x_minus + z_plus + z_minus + y_plus + y_minus - 6.0 * center
    forcing_term = jnp.array([FORCING, 0.0, 0.0], dtype=center.dtype)[:, None, None, None]
    return VISCOSITY * laplace - advect + forcing_term

def wall_term(values, stress, factor):
    values = values.at[0, :, 0, :].add(factor * stress[0, :, :, 0])
    values = values.at[2, :, 0, :].add(factor * stress[0, :, :, 1])
    values = values.at[0, :, -1, :].add(factor * stress[1, :, :, 0])
    values = values.at[2, :, -1, :].add(factor * stress[1, :, :, 1])
    return values

def tile_pass(tile_data, tile_targets, train_mask, w_one, w_two, w_three, loss_scale):
    flt = jnp.float32
    first_cols = patches(tile_data, 1).astype(flt)
    pre_one = jnp.einsum('sztk,skc->sztc', first_cols, w_one)
    hidden_one = jax.nn.silu(pre_one).astype(jnp.bfloat16)
    middle = patches(hidden_one, 1).astype(flt)
    pre_two = jnp.einsum('sztk,skc->sztc', middle, w_two)
    hidden_two = (jax.nn.silu(pre_two) + hidden_one.astype(flt)).astype(jnp.bfloat16)
    predicted = jnp.einsum('sztc,sco->szto', hidden_two.astype(flt), w_three)
    error_term = (2.0 * loss_scale * train_mask.astype(flt)[:, None, None, None] * (predicted - tile_targets.astype(flt))).astype(jnp.bfloat16)
    error_wide = error_term.astype(flt)
    grad_three = jnp.einsum('sztc,szto->sco', hidden_two.astype(flt), error_wide)
    grad_two_h = jnp.einsum('szto,sco->sztc', error_wide, w_three)
    grad_pre_two = (grad_two_h * silu_slope(pre_two)).astype(jnp.bfloat16)
    grad_two = jnp.einsum('sztk,sztc->skc', middle, grad_pre_two.astype(flt))
    chans = w_two.shape[2]
    turned = w_two.reshape(w_two.shape[0], 9, chans, chans).transpose(0, 1, 3, 2).reshape(w_two.shape[0], 9 * chans, chans)
    grad_one_h = grad_two_h + jnp.einsum('sztk,skc->sztc', patches(grad_pre_two, -1).astype(flt), turned)
    grad_pre_one = (grad_one_h * silu_slope(pre_one)).astype(jnp.bfloat16)
    grad_one = jnp.einsum('sztk,sztc->skc', first_cols, grad_pre_one.astype(flt))
    return (predicted, (grad_one, grad_two, grad_three))

def reference(velocity, target_stress, owner_map, train_order, w_first, w_mid, w_out):
    devices_all = N_LES * N_CNN
    tiles_along = CX // TX
    mirror = jnp.array([1.0, -1.0, 1.0], dtype=velocity.dtype)[:, None, None, None]
    bottom = velocity[:, :, :NPL, :]
    top = jnp.flip(velocity, axis=2)[:, :, :NPL, :] * mirror
    walls = jnp.stack([bottom, top]).reshape(2, 3, N_LES, CZ, NPL, N_CNN, tiles_along, TX)
    tile_data = walls.transpose(2, 5, 0, 6, 3, 7, 1, 4).reshape(devices_all, TILE_DEV, CZ, TX, 3 * NPL).astype(jnp.bfloat16)
    tile_targets = target_stress.reshape(2, N_LES, CZ, N_CNN, tiles_along, TX, 2).transpose(1, 3, 0, 4, 2, 5, 6).reshape(devices_all, TILE_DEV, CZ, TX, 2)
    train_mask = (train_order < TILE_DEV // 2).astype(jnp.bfloat16)
    owners = owner_map[:, 0].reshape(devices_all, TILE_DEV).astype(jnp.int32)
    loss_scale = 1.0 / math.sqrt(TX * CZ * TILE_DEV * N_CNN)

    def one_device(totals, inputs):
        data_now, targets_now, mask_now, owners_now = inputs
        predicted, grads = tile_pass(data_now, targets_now, mask_now, w_first[owners_now].astype(jnp.float32), w_mid[owners_now].astype(jnp.float32), w_out[owners_now].astype(jnp.float32), loss_scale)
        totals = tuple((total.at[owners_now].add(piece) for total, piece in zip(totals, grads)))
        return (totals, predicted)
    start = (jnp.zeros(w_first.shape, jnp.float32), jnp.zeros(w_mid.shape, jnp.float32), jnp.zeros(w_out.shape, jnp.float32))
    totals, predicted = lax.scan(one_device, start, (tile_data, tile_targets, train_mask, owners))
    wall_stress = predicted.reshape(N_LES, N_CNN, 2, tiles_along, CZ, TX, 2).transpose(2, 0, 4, 1, 3, 5, 6).reshape(2, N_LES * CZ, N_CNN * CX, 2)

    def one_slab(block_index):
        rows_index = ((block_index * CZ - 1 + jnp.arange(CZ + 2, dtype=jnp.int32)) % (N_LES * CZ)).astype(jnp.int32)
        z_slab = jnp.take(velocity, rows_index, axis=1)
        padded = jnp.concatenate([z_slab[..., -1:], z_slab, z_slab[..., :1]], axis=3)
        stress_now = lax.dynamic_slice_in_dim(wall_stress, (block_index * CZ).astype(jnp.int32), CZ, axis=1)
        change = wall_term(tendency(padded), stress_now, -1.0)
        return z_slab[:, 1:-1] + DT_STEP * change
    slabs = lax.map(one_slab, jnp.arange(N_LES, dtype=jnp.int32))
    new_velocity = slabs.transpose(1, 0, 2, 3, 4).reshape(velocity.shape)
    return (new_velocity, wall_stress, totals[0], totals[1], totals[2])
```

```python
import functools
import math

import jax
import jax.numpy as jnp
from jax import lax
from jax.experimental import pallas as pl
from jax.experimental.pallas import tpu as pltpu
from jax.sharding import PartitionSpec as P

TX = 4
NPL = 16
CZ = 2
NCNN = 4
C = 128
CIN = 48
CAP = 2
DT_STEP = 0.25
VISCOSITY = 0.05
FORCING = 0.2
GHOST = 8
LANES = 512
PRED = 128
MESH = pl.DeviceIdType.MESH
F32 = jnp.float32
BF16 = jnp.bfloat16


def z_extent(les_size):
    return 16 if les_size == 128 else 2


def dot(a, b):
    return lax.dot_general(a, b, (((1,), (0,)), ((), ())), preferred_element_type=F32)


def dot_nt(a, b):
    return lax.dot_general(a, b, (((1,), (1,)), ((), ())), preferred_element_type=F32)


def dot_tn(a, b):
    return lax.dot_general(a, b, (((0,), (0,)), ((), ())), preferred_element_type=F32)


def iota(shape, dim):
    return lax.broadcasted_iota(jnp.int32, shape, dim)


def log2(n):
    return n.bit_length() - 1


def gate(values):
    logistic = 0.5 * jnp.tanh(0.5 * values) + 0.5
    return values * logistic, logistic * (1.0 + values * (1.0 - logistic))


def kernel(
    own_ref, ord_ref, tgt_ref, wo_ref, vel_hbm, wf_hbm, wm_hbm,
    ws_ref, go_ref, nv_hbm, gf_hbm, gm_hbm,
    walls, v, nv, wf, wm, t_one, m_fwd, m_bwd, wo_t, sel,
    s1, x1, z0, z1, r0, r1, r2, r3, hs, hr, xs, xr,
    h_one, h_one_t, h_two, slope_one, slope_two, g_two, gp_two,
    m_part, m_in, m_send, m_got, m_tot, f_part, f_in, f_send, f_got, f_tot,
    local_sem, q_send, q_recv, zs_send, zs_recv, rz_send, rz_recv, rq_send, rq_recv,
    halo_send, halo_recv, grad_send, grad_recv,
):
    les_size = lax.axis_size("les")
    zn = z_extent(les_size)
    qn = les_size // zn
    rows = CAP * les_size
    _, _, ny, cx = vel_hbm.shape
    tiles = 2 * cx // TX
    both = 2 * cx
    loss_scale = 1.0 / math.sqrt(TX * CZ * tiles * NCNN)

    les, cnn = lax.axis_index("les"), lax.axis_index("cnn")
    z, q = les // qn, les % qn
    right, left = (les + 1) % les_size, (les + les_size - 1) % les_size
    east, west, across = (cnn + 1) % NCNN, (cnn + 3) % NCNN, (cnn + 2) % NCNN
    core = cnn % 2
    other = 1 - core
    twin = cnn + 1 - 2 * core

    def q_peer(step):
        return (q + step) % qn

    def z_peer(step):
        return (z + step) % zn

    far_first = sorted(range(1, zn), key=lambda s: -min(s, zn - s))

    barrier = pltpu.get_barrier_semaphore()
    greeted = 0
    for step in range(1, qn):
        pl.semaphore_signal(barrier, 1, device_id={"les": z * qn + q_peer(step)}, device_id_type=MESH)
        greeted += 1
    for step in range(1, zn):
        pl.semaphore_signal(barrier, 1, device_id={"les": z_peer(step) * qn + q}, device_id_type=MESH)
        greeted += 1
    for peer in (left, right):
        pl.semaphore_signal(barrier, 1, device_id={"les": peer}, device_id_type=MESH)
        greeted += 1
    for step in range(1, NCNN):
        pl.semaphore_signal(barrier, 1, device_id={"cnn": (cnn + step) % NCNN}, device_id_type=MESH)
        greeted += 1

    low_copy = pltpu.make_async_copy(vel_hbm.at[:, :, pl.ds(0, NPL), :], walls.at[0], local_sem.at[0])
    high_copy = pltpu.make_async_copy(vel_hbm.at[:, :, pl.ds(ny - NPL, NPL), :], walls.at[1], local_sem.at[1])
    v_copy = pltpu.make_async_copy(vel_hbm, v.at[:, :, pl.ds(GHOST, ny), :], local_sem.at[2])
    wf_copy = pltpu.make_async_copy(wf_hbm, wf, local_sem.at[3])
    wm_copy = pltpu.make_async_copy(wm_hbm, wm, local_sem.at[4])
    for copy in (low_copy, high_copy, v_copy, wf_copy, wm_copy):
        copy.start()

    own_row = own_ref[...].astype(F32)
    train_row = jnp.where(ord_ref[...] < tiles // 2, 1.0, 0.0)
    eye = iota((tiles, tiles), 0) == iota((tiles, tiles), 1)
    own_col = jnp.sum(jnp.where(eye, own_row, 0.0), axis=1, keepdims=True)
    train_col = jnp.sum(jnp.where(eye, train_row, 0.0), axis=1, keepdims=True)
    lane_tile = iota((tiles, both), 1) >> log2(TX)
    tile_row = iota((tiles, both), 0)
    hit = lane_tile == tile_row
    own_lane = jnp.sum(jnp.where(hit, own_col, 0.0), axis=0, keepdims=True)
    train_lane = jnp.sum(jnp.where(hit, train_col, 0.0), axis=0, keepdims=True)
    before = jnp.logical_and(own_col == own_lane, tile_row < lane_tile)
    rank_lane = jnp.sum(jnp.where(before, 1.0, 0.0), axis=0, keepdims=True).astype(jnp.int32)
    owner = own_lane.astype(jnp.int32)
    slot = (owner & (qn - 1)) * (CAP * zn) + (owner >> log2(qn)) * CAP + rank_lane
    sel[...] = jnp.where(iota((rows, both), 0) == slot, 1.0, 0.0).astype(BF16)

    low_copy.wait()
    high_copy.wait()
    planes = CZ * 3 * NPL
    order = [(zz, c) for zz in range(CZ) for c in range(3)]
    low = jnp.concatenate([walls[0, c, zz] for zz, c in order], axis=0).astype(BF16)
    high = jnp.concatenate([walls[1, c, zz] for zz, c in order], axis=0).astype(BF16)
    fr, fc = iota((planes, planes), 0), iota((planes, planes), 1)
    group = fr >> log2(NPL)
    turned = jnp.logical_and(group == (fc >> log2(NPL)), (fr & (NPL - 1)) + (fc & (NPL - 1)) == NPL - 1)
    sign = jnp.where(jnp.logical_or(group == 1, group == 4), -1.0, 1.0)
    flip = jnp.where(turned, sign, 0.0).astype(BF16)
    cells = jnp.concatenate([low.astype(F32), dot(flip, high)], axis=1)
    cell_x = iota((planes, both), 1) & (TX - 1)
    pieces = [jnp.where(cell_x == xx, cells, 0.0).astype(BF16) for xx in range(TX)]
    goal = [
        jnp.concatenate([tgt_ref[b, zz].astype(F32) for zz in range(CZ)], axis=0) for b in range(2)
    ]
    goal = jnp.concatenate(goal, axis=1)
    goal = jnp.concatenate([goal] * TX, axis=0)
    small_x = iota((16, both), 1) & (TX - 1)
    small_row = iota((16, both), 0)
    pieces.append(jnp.where(small_x == (small_row >> 2), goal, 0.0).astype(BF16))
    pieces.append(jnp.where(small_x == 0, jnp.broadcast_to(train_lane, (16, both)), 0.0).astype(BF16))
    pieces.append(jnp.zeros((LANES - TX * planes - 32, both), BF16))
    packed = dot_nt(sel[...], jnp.concatenate(pieces, axis=0)).astype(BF16)
    s1[...] = packed.reshape(qn, CAP * zn, LANES)

    pl.semaphore_wait(barrier, greeted)

    sends = []
    q_copies = []
    for step in range(1, qn):
        copy = pltpu.make_async_remote_copy(
            s1.at[q_peer(step)], x1.at[q], q_send.at[step], q_recv.at[step],
            device_id={"les": z * qn + q_peer(step)}, device_id_type=MESH,
        )
        copy.start()
        q_copies.append(copy)
    sends += q_copies
    x1[q] = s1[q]

    v_copy.wait()
    for zz in range(CZ):
        hs[zz] = v[:, zz, GHOST : GHOST + ny, :].astype(BF16)
    halo_copies = [
        pltpu.make_async_remote_copy(
            hs.at[1], hr.at[0], halo_send.at[0], halo_recv.at[0], device_id={"les": right}, device_id_type=MESH
        ),
        pltpu.make_async_remote_copy(
            hs.at[0], hr.at[1], halo_send.at[1], halo_recv.at[1], device_id={"les": left}, device_id_type=MESH
        ),
    ]
    for copy in halo_copies:
        copy.start()
    yl = xs.shape[2]
    per_column = ny // yl
    er, ec = iota((16, cx), 0), iota((16, cx), 1)
    first_or_last = jnp.logical_or(
        jnp.logical_and(er == 0, ec == 0), jnp.logical_and(er == 1, ec == cx - 1)
    )
    edges = jnp.where(first_or_last, 1.0, 0.0).astype(BF16)
    xs[...] = jnp.zeros(xs.shape, F32)
    for c in range(3):
        for zz in range(CZ):
            column = dot_nt(edges, hs[zz, c])
            for part in range(per_column):
                j = (c * CZ + zz) * per_column + part
                for side in range(2):
                    xs[side, j : j + 1, :] = column[side : side + 1, part * yl : (part + 1) * yl]
    x_copies = [
        pltpu.make_async_remote_copy(
            xs.at[1], xr.at[0], halo_send.at[2], halo_recv.at[2], device_id={"cnn": east}, device_id_type=MESH
        ),
        pltpu.make_async_remote_copy(
            xs.at[0], xr.at[1], halo_send.at[3], halo_recv.at[3], device_id={"cnn": west}, device_id_type=MESH
        ),
    ]
    for copy in x_copies:
        copy.start()
    sends += halo_copies + x_copies

    pr, pc = iota((rows, rows), 0), iota((rows, rows), 1)
    moved = ((pr >> 1) & (qn - 1)) * (CAP * zn) + (pr >> log2(CAP * qn)) * CAP + (pr & 1)
    to_z = jnp.where(pc == moved, 1.0, 0.0).astype(BF16)
    back = ((pr >> 1) & (zn - 1)) * (CAP * qn) + (pr >> log2(CAP * zn)) * CAP + (pr & 1)
    to_q = jnp.where(pc == back, 1.0, 0.0).astype(BF16)
    for copy in q_copies:
        copy.wait_recv()
    z0[...] = dot(to_z, x1[...].reshape(rows, LANES)).astype(BF16).reshape(zn, CAP * qn, LANES)
    z_copies = []
    for step in far_first:
        copy = pltpu.make_async_remote_copy(
            z0.at[z_peer(step)], z1.at[z], zs_send.at[step], zs_recv.at[step],
            device_id={"les": z_peer(step) * qn + q}, device_id_type=MESH,
        )
        copy.start()
        z_copies.append(copy)
    sends += z_copies
    z1[z] = z0[z]

    wf_copy.wait()
    wm_copy.wait()
    t_one[...] = jnp.zeros(t_one.shape, BF16)
    for xi in range(TX):
        for zi in range(CZ):
            for xo in range(max(0, xi - 1), min(TX, xi + 2)):
                for zo in range(CZ):
                    tap = 3 * (zi - zo + 1) + (xi - xo + 1)
                    at_row, at_lane = (xi * CZ + zi) * CIN, (xo * CZ + zo) * C
                    t_one[at_row : at_row + CIN, at_lane : at_lane + C] = wf[tap * CIN : (tap + 1) * CIN, :]
    wide = CZ * C
    for dx in (-1, 0, 1):
        for zi in range(CZ):
            for zo in range(CZ):
                tap = 3 * (zi - zo + 1) + (dx + 1)
                block = wm[tap * C : (tap + 1) * C, :]
                m_fwd[(dx + 1) * wide + zi * C : (dx + 1) * wide + (zi + 1) * C, zo * C : (zo + 1) * C] = block
                m_bwd[zi * C : (zi + 1) * C, (1 - dx) * wide + zo * C : (1 - dx) * wide + (zo + 1) * C] = block
    out_w = wo_ref[...].astype(F32)
    wr = iota((PRED, C), 0)
    for cell in range(TX * CZ):
        block = jnp.where(wr == 2 * cell, out_w[0:1], jnp.where(wr == 2 * cell + 1, out_w[1:2], 0.0))
        wo_t[:, cell * C : (cell + 1) * C] = block.astype(BF16)

    def near(x):
        return max(0, x - 1), min(TX, x + 2)

    for copy in z_copies:
        copy.wait_recv()

    got = z1[...].reshape(rows, LANES)
    data = got[:, : TX * planes]
    for x in range(TX):
        lanes = slice(x * wide, (x + 1) * wide)
        value, slope = gate(dot(data, t_one[:, lanes]))
        h_one[:, lanes] = value.astype(BF16)
        slope_one[:, lanes] = slope
    for x in range(TX):
        lanes = slice(x * wide, (x + 1) * wide)
        lo, hi = near(x)
        weights = m_fwd[(lo - x + 1) * wide : (hi - x + 1) * wide, :]
        value, slope = gate(dot(h_one[:, lo * wide : hi * wide], weights))
        h_two[:, lanes] = (value + h_one[:, lanes].astype(F32)).astype(BF16)
        slope_two[:, lanes] = slope
    predicted = dot_nt(h_two[...], wo_t[...])
    r0[...] = predicted.astype(BF16).reshape(zn, CAP * qn, PRED)
    rz_copies = []
    for step in far_first:
        copy = pltpu.make_async_remote_copy(
            r0.at[z_peer(step)], r1.at[z], rz_send.at[step], rz_recv.at[step],
            device_id={"les": z_peer(step) * qn + q}, device_id_type=MESH,
        )
        copy.start()
        rz_copies.append(copy)
    sends += rz_copies
    r1[z] = r0[z]

    extra = got[:, TX * planes : TX * planes + PRED].astype(F32)
    goal = jnp.where(iota((rows, PRED), 1) < 16, extra, 0.0)
    error = ((2.0 * loss_scale) * extra[:, 16:17] * (predicted - goal)).astype(BF16)
    for x in range(TX):
        lanes = slice(x * wide, (x + 1) * wide)
        grad = dot(error, wo_t[:, lanes])
        g_two[:, lanes] = grad
        gp_two[:, lanes] = (grad * slope_two[:, lanes]).astype(BF16)
    h_one_t[...] = h_one[...].T
    half_m = m_part.shape[1]

    def put_m(tap, value):
        start = tap * C
        while value.shape[0]:
            part, at = start // half_m, start % half_m
            take = min(value.shape[0], half_m - at)
            m_part[part, at : at + take, :] = value[:take]
            value, start = value[take:], start + take

    for dx in (-1, 0, 1):
        total = None
        for x in range(TX):
            if 0 <= x + dx < TX:
                term = dot(
                    h_one_t[(x + dx) * wide : (x + dx + 1) * wide, :], gp_two[:, x * wide : (x + 1) * wide]
                )
                total = term if total is None else total + term
        put_m(dx + 1, total[:C, C:])
        put_m(3 + dx + 1, total[:C, :C] + total[C:, C:])
        put_m(6 + dx + 1, total[C:, :C])

    def exchange(src, dst, index, peer):
        copy = pltpu.make_async_remote_copy(
            src, dst, grad_send.at[index], grad_recv.at[index], device_id={"cnn": peer}, device_id_type=MESH
        )
        copy.start()
        sends.append(copy)
        return copy

    m_first = exchange(m_part.at[other], m_in, 0, twin)

    data_t = data.T
    g_first = [None] * 9
    for x in range(TX):
        lanes = slice(x * wide, (x + 1) * wide)
        lo, hi = near(x)
        weights = m_bwd[:, (lo - x + 1) * wide : (hi - x + 1) * wide]
        grad = g_two[:, lanes] + dot_nt(gp_two[:, lo * wide : hi * wide], weights)
        gp_one = (grad * slope_one[:, lanes]).astype(BF16)
        lo_row, hi_row = lo * planes, hi * planes
        product = dot(data_t[lo_row:hi_row], gp_one)
        for xi in range(lo, hi):
            for zi in range(CZ):
                for zo in range(CZ):
                    tap = 3 * (zi - zo + 1) + (xi - x + 1)
                    at_row = (xi - lo) * planes + zi * CIN
                    piece = product[at_row : at_row + CIN, zo * C : (zo + 1) * C]
                    g_first[tap] = piece if g_first[tap] is None else g_first[tap] + piece
    half_f = f_part.shape[1]
    for tap in range(9):
        start, value = tap * CIN, g_first[tap]
        while value.shape[0]:
            part, at = start // half_f, start % half_f
            take = min(value.shape[0], half_f - at)
            f_part[part, at : at + take, :] = value[:take]
            value, start = value[take:], start + take
    cross = dot_tn(error, h_two[...])
    g_out = None
    for cell in range(TX * CZ):
        piece = cross[2 * cell : 2 * cell + 2, cell * C : (cell + 1) * C]
        g_out = piece if g_out is None else g_out + piece
    out_at = 9 * CIN - half_f
    f_part[1, out_at:half_f, :] = jnp.zeros((half_f - out_at, C), F32)
    f_part[1, out_at : out_at + 2, :] = g_out
    f_first = exchange(f_part.at[other], f_in, 1, twin)

    m_first.wait_recv()
    m_send[...] = (m_part[core] + m_in[...]).astype(BF16)
    m_second = exchange(m_send, m_got, 2, across)

    for copy in rz_copies:
        copy.wait_recv()
    r2[...] = dot(to_q, r1[...].reshape(rows, PRED)).astype(BF16).reshape(qn, CAP * zn, PRED)
    rq_copies = []
    for step in range(1, qn):
        copy = pltpu.make_async_remote_copy(
            r2.at[q_peer(step)], r3.at[q], rq_send.at[step], rq_recv.at[step],
            device_id={"les": z * qn + q_peer(step)}, device_id_type=MESH,
        )
        copy.start()
        rq_copies.append(copy)
    sends += rq_copies
    r3[q] = r2[q]

    f_first.wait_recv()
    f_send[...] = (f_part[core] + f_in[...]).astype(BF16)
    f_second = exchange(f_send, f_got, 3, across)

    for c in range(3):
        mirror = -1.0 if c == 1 else 1.0
        for zz in range(CZ):
            v[c, zz, GHOST - 1 : GHOST, :] = mirror * v[c, zz, GHOST : GHOST + 1, :]
            v[c, zz, GHOST + ny : GHOST + ny + 1, :] = mirror * v[c, zz, GHOST + ny - 1 : GHOST + ny, :]
    for copy in halo_copies + x_copies:
        copy.wait_recv()
    columns = [xr[side].T for side in range(2)]
    chunk = min(64, yl)
    lane = iota((chunk, cx), 1)
    for zz in range(CZ):
        for start in range(0, ny, chunk):
            here = slice(GHOST + start, GHOST + start + chunk)
            speed = [v[c, zz, here, :] for c in range(3)]
            for c in range(3):
                center = speed[c]
                j = (c * CZ + zz) * per_column + start // yl
                at = start % yl
                x_minus = jnp.where(
                    lane == 0, columns[0][at : at + chunk, j : j + 1], pltpu.roll(center, 1, 1)
                )
                x_plus = jnp.where(
                    lane == cx - 1, columns[1][at : at + chunk, j : j + 1], pltpu.roll(center, cx - 1, 1)
                )
                y_minus = v[c, zz, GHOST + start - 1 : GHOST + start - 1 + chunk, :]
                y_plus = v[c, zz, GHOST + start + 1 : GHOST + start + 1 + chunk, :]
                if zz == 0:
                    z_minus, z_plus = hr[0, c, start : start + chunk, :].astype(F32), v[c, 1, here, :]
                else:
                    z_minus, z_plus = v[c, 0, here, :], hr[1, c, start : start + chunk, :].astype(F32)
                advect = 0.5 * (
                    speed[0] * (x_plus - x_minus)
                    + speed[1] * (y_plus - y_minus)
                    + speed[2] * (z_plus - z_minus)
                )
                laplace = x_plus + x_minus + z_plus + z_minus + y_plus + y_minus - 6.0 * center
                change = VISCOSITY * laplace - advect
                if c == 0:
                    change = change + FORCING
                nv[c, zz, start : start + chunk, :] = center + DT_STEP * change

    m_second.wait_recv()
    m_tot[core] = m_send[...].astype(F32) + m_got[...].astype(F32)
    m_third = exchange(m_tot.at[core], m_tot.at[core], 4, twin)

    f_second.wait_recv()
    f_tot[core] = f_send[...].astype(F32) + f_got[...].astype(F32)
    f_third = exchange(f_tot.at[core], f_tot.at[core], 5, twin)

    for copy in rq_copies:
        copy.wait_recv()
    arrived = dot_tn(r3[...].reshape(rows, PRED), sel[...])
    wide_x = iota((2 * CZ, both), 1) & (TX - 1)
    stress = jnp.zeros((2 * CZ, both), F32)
    for xx in range(TX):
        stress = jnp.where(wide_x == xx, arrived[xx * 2 * CZ : (xx + 1) * 2 * CZ, :], stress)
    for b in range(2):
        row = 0 if b == 0 else ny - 1
        for zz in range(CZ):
            part = stress[zz * 2 : zz * 2 + 2, b * cx : (b + 1) * cx]
            ws_ref[b, zz] = part
            for m in range(2):
                c = 2 * m
                nv[c, zz, row : row + 1, :] = nv[c, zz, row : row + 1, :] - DT_STEP * part[m : m + 1]
    nv_copy = pltpu.make_async_copy(nv, nv_hbm, local_sem.at[5])
    nv_copy.start()

    m_third.wait_recv()
    gm_copy = pltpu.make_async_copy(m_tot, gm_hbm, local_sem.at[6])
    gm_copy.start()
    f_third.wait_recv()
    gf_low = pltpu.make_async_copy(f_tot.at[0], gf_hbm.at[pl.ds(0, half_f), :], local_sem.at[7])
    gf_high = pltpu.make_async_copy(
        f_tot.at[1, pl.ds(0, out_at), :], gf_hbm.at[pl.ds(half_f, out_at), :], local_sem.at[8]
    )
    gf_low.start()
    gf_high.start()
    go_ref[...] = f_tot[1, out_at : out_at + 2, :]
    for copy in sends:
        copy.wait_send()
    for copy in (nv_copy, gm_copy, gf_low, gf_high):
        copy.wait()


def per_device(velocity, target_stress, owner_map, train_order, w_first, w_mid, w_out):
    les_size = lax.axis_size("les")
    zn = z_extent(les_size)
    qn = les_size // zn
    rows = CAP * les_size
    _, _, ny, cx = velocity.shape
    tiles = owner_map.shape[0]
    hidden = TX * CZ * C
    half_m, half_f = 9 * C // 2, 224
    yl = min(128, ny)
    vmem = pltpu.VMEM
    scratch = [
        vmem((2, 3, CZ, NPL, cx), F32),
        vmem((3, CZ, ny + 2 * GHOST, cx), F32),
        vmem((3, CZ, ny, cx), F32),
        vmem((9 * CIN, C), BF16),
        vmem((9 * C, C), BF16),
        vmem((TX * CZ * CIN, hidden), BF16),
        vmem((3 * CZ * C, CZ * C), BF16),
        vmem((CZ * C, 3 * CZ * C), BF16),
        vmem((PRED, hidden), BF16),
        vmem((rows, 2 * cx), BF16),
        vmem((qn, CAP * zn, LANES), BF16),
        vmem((qn, CAP * zn, LANES), BF16),
        vmem((zn, CAP * qn, LANES), BF16),
        vmem((zn, CAP * qn, LANES), BF16),
        vmem((zn, CAP * qn, PRED), BF16),
        vmem((zn, CAP * qn, PRED), BF16),
        vmem((qn, CAP * zn, PRED), BF16),
        vmem((qn, CAP * zn, PRED), BF16),
        vmem((CZ, 3, ny, cx), BF16),
        vmem((CZ, 3, ny, cx), BF16),
        vmem((2, 16, yl), F32),
        vmem((2, 16, yl), F32),
        vmem((rows, hidden), BF16),
        vmem((hidden, rows), BF16),
        vmem((rows, hidden), BF16),
        vmem((rows, hidden), F32),
        vmem((rows, hidden), F32),
        vmem((rows, hidden), F32),
        vmem((rows, hidden), BF16),
        vmem((2, half_m, C), F32),
        vmem((half_m, C), F32),
        vmem((half_m, C), BF16),
        vmem((half_m, C), BF16),
        vmem((2, half_m, C), F32),
        vmem((2, half_f, C), F32),
        vmem((half_f, C), F32),
        vmem((half_f, C), BF16),
        vmem((half_f, C), BF16),
        vmem((2, half_f, C), F32),
        pltpu.SemaphoreType.DMA((9,)),
        pltpu.SemaphoreType.DMA((qn,)),
        pltpu.SemaphoreType.DMA((qn,)),
        pltpu.SemaphoreType.DMA((zn,)),
        pltpu.SemaphoreType.DMA((zn,)),
        pltpu.SemaphoreType.DMA((zn,)),
        pltpu.SemaphoreType.DMA((zn,)),
        pltpu.SemaphoreType.DMA((qn,)),
        pltpu.SemaphoreType.DMA((qn,)),
        pltpu.SemaphoreType.DMA((4,)),
        pltpu.SemaphoreType.DMA((4,)),
        pltpu.SemaphoreType.DMA((6,)),
        pltpu.SemaphoreType.DMA((6,)),
    ]
    in_vmem = pl.BlockSpec(memory_space=pltpu.VMEM)
    anywhere = pl.BlockSpec(memory_space=pl.ANY)
    stress, grad_out, new_velocity, grad_first, grad_mid = pl.pallas_call(
        kernel,
        out_shape=(
            jax.ShapeDtypeStruct((2, CZ, 2, cx), F32),
            jax.ShapeDtypeStruct((2, C), F32),
            jax.ShapeDtypeStruct(velocity.shape, F32),
            jax.ShapeDtypeStruct((9 * CIN, C), F32),
            jax.ShapeDtypeStruct((2, half_m, C), F32),
        ),
        in_specs=[in_vmem] * 4 + [anywhere] * 3,
        out_specs=(in_vmem, in_vmem, anywhere, anywhere, anywhere),
        scratch_shapes=scratch,
        compiler_params=pltpu.CompilerParams(
            collective_id=0, has_side_effects=True, vmem_limit_bytes=60 * 2**20
        ),
    )(
        owner_map.reshape(1, tiles),
        train_order,
        target_stress.transpose(0, 1, 3, 2),
        w_out[0].T,
        velocity,
        w_first[0],
        w_mid[0],
    )
    return (
        new_velocity,
        stress.transpose(0, 1, 3, 2),
        grad_first[None],
        grad_mid.reshape(1, 9 * C, C),
        grad_out.T[None],
    )


def solution(mesh):
    placed = (
        P(None, "les", None, "cnn"),
        P(None, "les", "cnn", None),
        P(("les", "cnn"), None),
        P(("les", "cnn"), None),
        P("les", None, None),
        P("les", None, None),
        P("les", None, None),
    )
    return jax.shard_map(
        per_device,
        mesh=mesh,
        in_specs=placed,
        out_specs=(
            P(None, "les", None, "cnn"),
            P(None, "les", "cnn", None),
            P("les", None, None),
            P("les", None, None),
            P("les", None, None),
        ),
        check_vma=False,
    )
```

```python
import functools
import math

import jax
import jax.numpy as jnp
from jax import lax
from jax.experimental import pallas as pl
from jax.experimental.pallas import tpu as pltpu
from jax.sharding import PartitionSpec as P

TX = 4
NPL = 16
CZ = 2
NCNN = 4
C = 128
CIN = 48
CAP = 2
DT_STEP = 0.25
VISCOSITY = 0.05
FORCING = 0.2
GHOST = 8
DATA = TX * CZ * CIN
PRED = 128
MESH = pl.DeviceIdType.MESH
F32 = jnp.float32
BF16 = jnp.bfloat16


def z_extent(les_size):
    return 16 if les_size == 128 else 2


def dot(a, b):
    return lax.dot_general(a, b, (((1,), (0,)), ((), ())), preferred_element_type=F32)


def dot_nt(a, b):
    return lax.dot_general(a, b, (((1,), (1,)), ((), ())), preferred_element_type=F32)


def dot_tn(a, b):
    return lax.dot_general(a, b, (((0,), (0,)), ((), ())), preferred_element_type=F32)


def iota(shape, dim):
    return lax.broadcasted_iota(jnp.int32, shape, dim)


def log2(n):
    return n.bit_length() - 1


def gate(values):
    logistic = 0.5 * jnp.tanh(0.5 * values) + 0.5
    return values * logistic, logistic * (1.0 + values * (1.0 - logistic))


def kernel(
    own_hbm, ord_hbm, tgt_hbm, wo_hbm, vel_hbm, wf_hbm, wm_hbm,
    ws_hbm, go_hbm, nv_hbm, gf_hbm, gm_hbm,
    own_ref, ord_ref, tgt_ref, wo_ref, ws_ref, go_ref,
    walls, v, nv, wf, wm, t_one, m_fwd, m_bwd, wo_t, sel,
    s1, x1, z0, z1, s1_more, x1_more, z0_more, z1_more, r0, r1, r2, r3, hs, hr, xs, xr,
    h_one, h_one_t, h_two, slope_one, slope_two, g_two, gp_two,
    m_part, m_in, m_send, m_got, m_tot, f_part, f_in, f_send, f_got, f_tot,
    local_sem, q_send, q_recv, qm_send, qm_recv, zs_send, zs_recv, zm_send, zm_recv,
    rz_send, rz_recv, rq_send, rq_recv,
    halo_send, halo_recv, grad_send, grad_recv,
):
    les_size = lax.axis_size("les")
    zn = z_extent(les_size)
    qn = les_size // zn
    rows = CAP * les_size
    _, _, ny, cx = vel_hbm.shape
    tiles = 2 * cx // TX
    both = 2 * cx
    loss_scale = 1.0 / math.sqrt(TX * CZ * tiles * NCNN)

    les, cnn = lax.axis_index("les"), lax.axis_index("cnn")
    z, q = les // qn, les % qn
    right, left = (les + 1) % les_size, (les + les_size - 1) % les_size
    east, west, across = (cnn + 1) % NCNN, (cnn + 3) % NCNN, (cnn + 2) % NCNN
    core = cnn % 2
    other = 1 - core
    twin = cnn + 1 - 2 * core

    def q_peer(step):
        return (q + step) % qn

    def z_peer(step):
        return (z + step) % zn

    far_first = sorted(range(1, zn), key=lambda s: -min(s, zn - s))
    q_order = list(range(1, qn))

    barrier = pltpu.get_barrier_semaphore()
    greeted = 0
    for step in range(1, qn):
        pl.semaphore_signal(barrier, 1, device_id={"les": z * qn + q_peer(step)}, device_id_type=MESH)
        greeted += 1
    for step in range(1, zn):
        pl.semaphore_signal(barrier, 1, device_id={"les": z_peer(step) * qn + q}, device_id_type=MESH)
        greeted += 1
    for peer in (left, right):
        pl.semaphore_signal(barrier, 1, device_id={"les": peer}, device_id_type=MESH)
        greeted += 1
    for step in range(1, NCNN):
        pl.semaphore_signal(barrier, 1, device_id={"cnn": (cnn + step) % NCNN}, device_id_type=MESH)
        greeted += 1

    low_copy = pltpu.make_async_copy(vel_hbm.at[:, :, pl.ds(0, NPL), :], walls.at[0], local_sem.at[0])
    high_copy = pltpu.make_async_copy(vel_hbm.at[:, :, pl.ds(ny - NPL, NPL), :], walls.at[1], local_sem.at[1])
    v_copy = pltpu.make_async_copy(vel_hbm, v.at[:, :, pl.ds(GHOST, ny), :], local_sem.at[2])
    wf_copy = pltpu.make_async_copy(wf_hbm, wf, local_sem.at[3])
    wm_copy = pltpu.make_async_copy(wm_hbm, wm, local_sem.at[4])
    small_copies = [
        pltpu.make_async_copy(src, dst, local_sem.at[9 + i])
        for i, (src, dst) in enumerate(
            ((own_hbm, own_ref), (ord_hbm, ord_ref), (tgt_hbm, tgt_ref), (wo_hbm, wo_ref))
        )
    ]
    for copy in small_copies + [low_copy, high_copy, v_copy, wf_copy, wm_copy]:
        copy.start()
    for copy in small_copies:
        copy.wait()

    own_row = own_ref[...].astype(F32)
    train_row = jnp.where(ord_ref[...] < tiles // 2, 1.0, 0.0)
    eye = iota((tiles, tiles), 0) == iota((tiles, tiles), 1)
    own_col = jnp.sum(jnp.where(eye, own_row, 0.0), axis=1, keepdims=True)
    train_col = jnp.sum(jnp.where(eye, train_row, 0.0), axis=1, keepdims=True)
    lane_tile = iota((tiles, both), 1) >> log2(TX)
    tile_row = iota((tiles, both), 0)
    hit = lane_tile == tile_row
    own_lane = jnp.sum(jnp.where(hit, own_col, 0.0), axis=0, keepdims=True)
    train_lane = jnp.sum(jnp.where(hit, train_col, 0.0), axis=0, keepdims=True)
    before = jnp.logical_and(own_col == own_lane, tile_row < lane_tile)
    rank_lane = jnp.sum(jnp.where(before, 1.0, 0.0), axis=0, keepdims=True).astype(jnp.int32)
    owner = own_lane.astype(jnp.int32)
    slot = (owner & (qn - 1)) * (CAP * zn) + (owner >> log2(qn)) * CAP + rank_lane
    sel[...] = jnp.where(iota((rows, both), 0) == slot, 1.0, 0.0).astype(BF16)

    low_copy.wait()
    high_copy.wait()
    planes = CZ * 3 * NPL
    order = [(zz, c) for zz in range(CZ) for c in range(3)]
    low = jnp.concatenate([walls[0, c, zz] for zz, c in order], axis=0).astype(BF16)
    high = jnp.concatenate([walls[1, c, zz] for zz, c in order], axis=0).astype(BF16)
    fr, fc = iota((planes, planes), 0), iota((planes, planes), 1)
    group = fr >> log2(NPL)
    turned = jnp.logical_and(group == (fc >> log2(NPL)), (fr & (NPL - 1)) + (fc & (NPL - 1)) == NPL - 1)
    sign = jnp.where(jnp.logical_or(group == 1, group == 4), -1.0, 1.0)
    flip = jnp.where(turned, sign, 0.0).astype(BF16)
    cells = jnp.concatenate([low.astype(F32), dot(flip, high)], axis=1)
    cell_x = iota((planes, both), 1) & (TX - 1)
    pieces = [jnp.where(cell_x == xx, cells, 0.0).astype(BF16) for xx in range(TX)]
    goal = [
        jnp.concatenate([tgt_ref[b, zz].astype(F32) for zz in range(CZ)], axis=0) for b in range(2)
    ]
    goal = jnp.concatenate(goal, axis=1)
    goal = jnp.concatenate([goal] * TX, axis=0)
    small_x = iota((16, both), 1) & (TX - 1)
    small_row = iota((16, both), 0)
    more = [
        jnp.where(small_x == (small_row >> 2), goal, 0.0).astype(BF16),
        jnp.where(small_x == 0, jnp.broadcast_to(train_lane, (16, both)), 0.0).astype(BF16),
        jnp.zeros((PRED - 32, both), BF16),
    ]
    packed = dot_nt(sel[...], jnp.concatenate(pieces, axis=0)).astype(BF16)
    s1[...] = packed.reshape(qn, CAP * zn, DATA)
    packed = dot_nt(sel[...], jnp.concatenate(more, axis=0)).astype(BF16)
    s1_more[...] = packed.reshape(qn, CAP * zn, PRED)

    pl.semaphore_wait(barrier, greeted)

    sends = []

    def spread_q(src, dst, send_sem, recv_sem):
        copies = []
        for step in q_order:
            copy = pltpu.make_async_remote_copy(
                src.at[q_peer(step)], dst.at[q], send_sem.at[step], recv_sem.at[step],
                device_id={"les": z * qn + q_peer(step)}, device_id_type=MESH,
            )
            copy.start()
            copies.append(copy)
        sends.extend(copies)
        dst[q] = src[q]
        return copies

    def spread_z(src, dst, send_sem, recv_sem):
        copies = []
        for step in far_first:
            copy = pltpu.make_async_remote_copy(
                src.at[z_peer(step)], dst.at[z], send_sem.at[step], recv_sem.at[step],
                device_id={"les": z_peer(step) * qn + q}, device_id_type=MESH,
            )
            copy.start()
            copies.append(copy)
        sends.extend(copies)
        dst[z] = src[z]
        return copies

    q_copies = spread_q(s1, x1, q_send, q_recv)
    qm_copies = spread_q(s1_more, x1_more, qm_send, qm_recv)

    v_copy.wait()
    for zz in range(CZ):
        hs[zz] = v[:, zz, GHOST : GHOST + ny, :].astype(BF16)
    halo_copies = [
        pltpu.make_async_remote_copy(
            hs.at[1], hr.at[0], halo_send.at[0], halo_recv.at[0], device_id={"les": right}, device_id_type=MESH
        ),
        pltpu.make_async_remote_copy(
            hs.at[0], hr.at[1], halo_send.at[1], halo_recv.at[1], device_id={"les": left}, device_id_type=MESH
        ),
    ]
    yl = xs.shape[2]
    per_column = ny // yl
    er, ec = iota((16, cx), 0), iota((16, cx), 1)
    first_or_last = jnp.logical_or(
        jnp.logical_and(er == 0, ec == 0), jnp.logical_and(er == 1, ec == cx - 1)
    )
    edges = jnp.where(first_or_last, 1.0, 0.0).astype(BF16)
    xs[...] = jnp.zeros(xs.shape, F32)
    for c in range(3):
        for zz in range(CZ):
            column = dot_nt(edges, hs[zz, c])
            for part in range(per_column):
                j = (c * CZ + zz) * per_column + part
                for side in range(2):
                    xs[side, j : j + 1, :] = column[side : side + 1, part * yl : (part + 1) * yl]
    x_copies = [
        pltpu.make_async_remote_copy(
            xs.at[1], xr.at[0], halo_send.at[2], halo_recv.at[2], device_id={"cnn": east}, device_id_type=MESH
        ),
        pltpu.make_async_remote_copy(
            xs.at[0], xr.at[1], halo_send.at[3], halo_recv.at[3], device_id={"cnn": west}, device_id_type=MESH
        ),
    ]

    pr, pc = iota((rows, rows), 0), iota((rows, rows), 1)
    moved = ((pr >> 1) & (qn - 1)) * (CAP * zn) + (pr >> log2(CAP * qn)) * CAP + (pr & 1)
    to_z = jnp.where(pc == moved, 1.0, 0.0).astype(BF16)
    back = ((pr >> 1) & (zn - 1)) * (CAP * qn) + (pr >> log2(CAP * zn)) * CAP + (pr & 1)
    to_q = jnp.where(pc == back, 1.0, 0.0).astype(BF16)
    for copy in q_copies:
        copy.wait_recv()
    z0[...] = dot(to_z, x1[...].reshape(rows, DATA)).astype(BF16).reshape(zn, CAP * qn, DATA)
    z_copies = spread_z(z0, z1, zs_send, zs_recv)
    for copy in qm_copies:
        copy.wait_recv()
    z0_more[...] = dot(to_z, x1_more[...].reshape(rows, PRED)).astype(BF16).reshape(zn, CAP * qn, PRED)
    zm_copies = spread_z(z0_more, z1_more, zm_send, zm_recv)
    for copy in halo_copies + x_copies:
        copy.start()
    sends.extend(halo_copies + x_copies)

    wf_copy.wait()
    wm_copy.wait()
    t_one[...] = jnp.zeros(t_one.shape, BF16)
    for xi in range(TX):
        for zi in range(CZ):
            for xo in range(max(0, xi - 1), min(TX, xi + 2)):
                for zo in range(CZ):
                    tap = 3 * (zi - zo + 1) + (xi - xo + 1)
                    at_row, at_lane = (xi * CZ + zi) * CIN, (xo * CZ + zo) * C
                    t_one[at_row : at_row + CIN, at_lane : at_lane + C] = wf[tap * CIN : (tap + 1) * CIN, :]
    wide = CZ * C
    for dx in (-1, 0, 1):
        for zi in range(CZ):
            for zo in range(CZ):
                tap = 3 * (zi - zo + 1) + (dx + 1)
                block = wm[tap * C : (tap + 1) * C, :]
                m_fwd[(dx + 1) * wide + zi * C : (dx + 1) * wide + (zi + 1) * C, zo * C : (zo + 1) * C] = block
                m_bwd[zi * C : (zi + 1) * C, (1 - dx) * wide + zo * C : (1 - dx) * wide + (zo + 1) * C] = block
    out_w = wo_ref[...].astype(F32)
    wr = iota((PRED, C), 0)
    for cell in range(TX * CZ):
        block = jnp.where(wr == 2 * cell, out_w[0:1], jnp.where(wr == 2 * cell + 1, out_w[1:2], 0.0))
        wo_t[:, cell * C : (cell + 1) * C] = block.astype(BF16)

    def near(x):
        return max(0, x - 1), min(TX, x + 2)

    for copy in z_copies:
        copy.wait_recv()

    data = z1[...].reshape(rows, DATA)
    for x in range(TX):
        lanes = slice(x * wide, (x + 1) * wide)
        value, slope = gate(dot(data, t_one[:, lanes]))
        h_one[:, lanes] = value.astype(BF16)
        slope_one[:, lanes] = slope
    for x in range(TX):
        lanes = slice(x * wide, (x + 1) * wide)
        lo, hi = near(x)
        weights = m_fwd[(lo - x + 1) * wide : (hi - x + 1) * wide, :]
        value, slope = gate(dot(h_one[:, lo * wide : hi * wide], weights))
        h_two[:, lanes] = (value + h_one[:, lanes].astype(F32)).astype(BF16)
        slope_two[:, lanes] = slope
    predicted = dot_nt(h_two[...], wo_t[...])
    r0[...] = predicted.astype(BF16).reshape(zn, CAP * qn, PRED)
    rz_copies = spread_z(r0, r1, rz_send, rz_recv)

    for copy in zm_copies:
        copy.wait_recv()
    extra = z1_more[...].reshape(rows, PRED).astype(F32)
    goal = jnp.where(iota((rows, PRED), 1) < 16, extra, 0.0)
    error = ((2.0 * loss_scale) * extra[:, 16:17] * (predicted - goal)).astype(BF16)
    for x in range(TX):
        lanes = slice(x * wide, (x + 1) * wide)
        grad = dot(error, wo_t[:, lanes])
        g_two[:, lanes] = grad
        gp_two[:, lanes] = (grad * slope_two[:, lanes]).astype(BF16)
    h_one_t[...] = h_one[...].T
    half_m = m_part.shape[1]

    def put_m(tap, value):
        start = tap * C
        while value.shape[0]:
            part, at = start // half_m, start % half_m
            take = min(value.shape[0], half_m - at)
            m_part[part, at : at + take, :] = value[:take]
            value, start = value[take:], start + take

    for dx in (-1, 0, 1):
        total = None
        for x in range(TX):
            if 0 <= x + dx < TX:
                term = dot(
                    h_one_t[(x + dx) * wide : (x + dx + 1) * wide, :], gp_two[:, x * wide : (x + 1) * wide]
                )
                total = term if total is None else total + term
        put_m(dx + 1, total[:C, C:])
        put_m(3 + dx + 1, total[:C, :C] + total[C:, C:])
        put_m(6 + dx + 1, total[C:, :C])

    def exchange(src, dst, index, peer):
        copy = pltpu.make_async_remote_copy(
            src, dst, grad_send.at[index], grad_recv.at[index], device_id={"cnn": peer}, device_id_type=MESH
        )
        copy.start()
        sends.append(copy)
        return copy

    m_first = exchange(m_part.at[other], m_in, 0, twin)

    data_t = data.T
    g_first = [None] * 9
    for x in range(TX):
        lanes = slice(x * wide, (x + 1) * wide)
        lo, hi = near(x)
        weights = m_bwd[:, (lo - x + 1) * wide : (hi - x + 1) * wide]
        grad = g_two[:, lanes] + dot_nt(gp_two[:, lo * wide : hi * wide], weights)
        gp_one = (grad * slope_one[:, lanes]).astype(BF16)
        lo_row, hi_row = lo * planes, hi * planes
        product = dot(data_t[lo_row:hi_row], gp_one)
        for xi in range(lo, hi):
            for zi in range(CZ):
                for zo in range(CZ):
                    tap = 3 * (zi - zo + 1) + (xi - x + 1)
                    at_row = (xi - lo) * planes + zi * CIN
                    piece = product[at_row : at_row + CIN, zo * C : (zo + 1) * C]
                    g_first[tap] = piece if g_first[tap] is None else g_first[tap] + piece
    half_f = f_part.shape[1]
    for tap in range(9):
        start, value = tap * CIN, g_first[tap]
        while value.shape[0]:
            part, at = start // half_f, start % half_f
            take = min(value.shape[0], half_f - at)
            f_part[part, at : at + take, :] = value[:take]
            value, start = value[take:], start + take
    cross = dot_tn(error, h_two[...])
    g_out = None
    for cell in range(TX * CZ):
        piece = cross[2 * cell : 2 * cell + 2, cell * C : (cell + 1) * C]
        g_out = piece if g_out is None else g_out + piece
    out_at = 9 * CIN - half_f
    f_part[1, out_at:half_f, :] = jnp.zeros((half_f - out_at, C), F32)
    f_part[1, out_at : out_at + 2, :] = g_out
    f_first = exchange(f_part.at[other], f_in, 1, twin)

    m_first.wait_recv()
    m_send[...] = (m_part[core] + m_in[...]).astype(BF16)
    m_second = exchange(m_send, m_got, 2, across)

    for copy in rz_copies:
        copy.wait_recv()
    r2[...] = dot(to_q, r1[...].reshape(rows, PRED)).astype(BF16).reshape(qn, CAP * zn, PRED)
    rq_copies = spread_q(r2, r3, rq_send, rq_recv)

    f_first.wait_recv()
    f_send[...] = (f_part[core] + f_in[...]).astype(BF16)
    f_second = exchange(f_send, f_got, 3, across)

    for c in range(3):
        mirror = -1.0 if c == 1 else 1.0
        for zz in range(CZ):
            v[c, zz, GHOST - 1 : GHOST, :] = mirror * v[c, zz, GHOST : GHOST + 1, :]
            v[c, zz, GHOST + ny : GHOST + ny + 1, :] = mirror * v[c, zz, GHOST + ny - 1 : GHOST + ny, :]
    for copy in halo_copies + x_copies:
        copy.wait_recv()
    columns = [xr[side].T for side in range(2)]
    chunk = min(64, yl)
    lane = iota((chunk, cx), 1)
    for zz in range(CZ):
        for start in range(0, ny, chunk):
            here = slice(GHOST + start, GHOST + start + chunk)
            speed = [v[c, zz, here, :] for c in range(3)]
            for c in range(3):
                center = speed[c]
                j = (c * CZ + zz) * per_column + start // yl
                at = start % yl
                x_minus = jnp.where(
                    lane == 0, columns[0][at : at + chunk, j : j + 1], pltpu.roll(center, 1, 1)
                )
                x_plus = jnp.where(
                    lane == cx - 1, columns[1][at : at + chunk, j : j + 1], pltpu.roll(center, cx - 1, 1)
                )
                y_minus = v[c, zz, GHOST + start - 1 : GHOST + start - 1 + chunk, :]
                y_plus = v[c, zz, GHOST + start + 1 : GHOST + start + 1 + chunk, :]
                if zz == 0:
                    z_minus, z_plus = hr[0, c, start : start + chunk, :].astype(F32), v[c, 1, here, :]
                else:
                    z_minus, z_plus = v[c, 0, here, :], hr[1, c, start : start + chunk, :].astype(F32)
                advect = 0.5 * (
                    speed[0] * (x_plus - x_minus)
                    + speed[1] * (y_plus - y_minus)
                    + speed[2] * (z_plus - z_minus)
                )
                laplace = x_plus + x_minus + z_plus + z_minus + y_plus + y_minus - 6.0 * center
                change = VISCOSITY * laplace - advect
                if c == 0:
                    change = change + FORCING
                nv[c, zz, start : start + chunk, :] = center + DT_STEP * change

    rim = 8
    body = pltpu.make_async_copy(
        nv.at[:, :, pl.ds(rim, ny - 2 * rim), :], nv_hbm.at[:, :, pl.ds(rim, ny - 2 * rim), :], local_sem.at[5]
    )
    body.start()

    m_second.wait_recv()
    m_tot[core] = m_send[...].astype(F32) + m_got[...].astype(F32)
    m_third = exchange(m_tot.at[core], m_tot.at[core], 4, twin)

    f_second.wait_recv()
    f_tot[core] = f_send[...].astype(F32) + f_got[...].astype(F32)
    f_third = exchange(f_tot.at[core], f_tot.at[core], 5, twin)

    for copy in rq_copies:
        copy.wait_recv()
    arrived = dot_tn(r3[...].reshape(rows, PRED), sel[...])
    wide_x = iota((2 * CZ, both), 1) & (TX - 1)
    stress = jnp.zeros((2 * CZ, both), F32)
    for xx in range(TX):
        stress = jnp.where(wide_x == xx, arrived[xx * 2 * CZ : (xx + 1) * 2 * CZ, :], stress)
    for b in range(2):
        row = 0 if b == 0 else ny - 1
        for zz in range(CZ):
            part = stress[zz * 2 : zz * 2 + 2, b * cx : (b + 1) * cx]
            ws_ref[b, zz] = part
            for m in range(2):
                c = 2 * m
                nv[c, zz, row : row + 1, :] = nv[c, zz, row : row + 1, :] - DT_STEP * part[m : m + 1]
    rims = [
        pltpu.make_async_copy(
            nv.at[:, :, pl.ds(at, rim), :], nv_hbm.at[:, :, pl.ds(at, rim), :], local_sem.at[13 + i]
        )
        for i, at in enumerate((0, ny - rim))
    ]
    rims.append(pltpu.make_async_copy(ws_ref, ws_hbm, local_sem.at[15]))
    for copy in rims:
        copy.start()

    m_third.wait_recv()
    gm_copy = pltpu.make_async_copy(m_tot, gm_hbm, local_sem.at[6])
    gm_copy.start()
    f_third.wait_recv()
    gf_low = pltpu.make_async_copy(f_tot.at[0], gf_hbm.at[pl.ds(0, half_f), :], local_sem.at[7])
    gf_high = pltpu.make_async_copy(
        f_tot.at[1, pl.ds(0, out_at), :], gf_hbm.at[pl.ds(half_f, out_at), :], local_sem.at[8]
    )
    gf_low.start()
    gf_high.start()
    go_ref[...] = f_tot[1, out_at : out_at + 2, :]
    go_copy = pltpu.make_async_copy(go_ref, go_hbm, local_sem.at[16])
    go_copy.start()
    for copy in sends:
        copy.wait_send()
    for copy in rims + [body, gm_copy, gf_low, gf_high, go_copy]:
        copy.wait()


def hand_on(*refs):
    count = (len(refs) - 2) // 3
    given, results, held = refs[:count], refs[count : 2 * count], refs[2 * count : 3 * count]
    into, out = refs[-2:]
    parts = [(i, k) for i in range(count) for k in range(given[i].shape[0] if given[i].shape[0] == 3 else 1)]

    def pick(ref, k):
        return ref.at[k] if ref.shape[0] == 3 else ref

    loads = [
        pltpu.make_async_copy(pick(given[i], k), pick(held[i], k), into.at[n]) for n, (i, k) in enumerate(parts)
    ]
    stores = [
        pltpu.make_async_copy(pick(held[i], k), pick(results[i], k), out.at[n]) for n, (i, k) in enumerate(parts)
    ]
    for load in loads:
        load.start()
    for load, store in zip(loads, stores):
        load.wait()
        store.start()
    for store in stores:
        store.wait()


def per_device(velocity, target_stress, owner_map, train_order, w_first, w_mid, w_out):
    les_size = lax.axis_size("les")
    zn = z_extent(les_size)
    qn = les_size // zn
    rows = CAP * les_size
    _, _, ny, cx = velocity.shape
    tiles = owner_map.shape[0]
    hidden = TX * CZ * C
    half_m, half_f = 9 * C // 2, 224
    yl = min(128, ny)
    vmem = pltpu.VMEM
    scratch = [
        vmem((1, tiles), jnp.int32),
        vmem((1, tiles), jnp.int32),
        vmem((2, CZ, 2, cx), BF16),
        vmem((2, C), BF16),
        vmem((2, CZ, 2, cx), F32),
        vmem((2, C), F32),
        vmem((2, 3, CZ, NPL, cx), F32),
        vmem((3, CZ, ny + 2 * GHOST, cx), F32),
        vmem((3, CZ, ny, cx), F32),
        vmem((9 * CIN, C), BF16),
        vmem((9 * C, C), BF16),
        vmem((TX * CZ * CIN, hidden), BF16),
        vmem((3 * CZ * C, CZ * C), BF16),
        vmem((CZ * C, 3 * CZ * C), BF16),
        vmem((PRED, hidden), BF16),
        vmem((rows, 2 * cx), BF16),
        vmem((qn, CAP * zn, DATA), BF16),
        vmem((qn, CAP * zn, DATA), BF16),
        vmem((zn, CAP * qn, DATA), BF16),
        vmem((zn, CAP * qn, DATA), BF16),
        vmem((qn, CAP * zn, PRED), BF16),
        vmem((qn, CAP * zn, PRED), BF16),
        vmem((zn, CAP * qn, PRED), BF16),
        vmem((zn, CAP * qn, PRED), BF16),
        vmem((zn, CAP * qn, PRED), BF16),
        vmem((zn, CAP * qn, PRED), BF16),
        vmem((qn, CAP * zn, PRED), BF16),
        vmem((qn, CAP * zn, PRED), BF16),
        vmem((CZ, 3, ny, cx), BF16),
        vmem((CZ, 3, ny, cx), BF16),
        vmem((2, 16, yl), F32),
        vmem((2, 16, yl), F32),
        vmem((rows, hidden), BF16),
        vmem((hidden, rows), BF16),
        vmem((rows, hidden), BF16),
        vmem((rows, hidden), F32),
        vmem((rows, hidden), F32),
        vmem((rows, hidden), F32),
        vmem((rows, hidden), BF16),
        vmem((2, half_m, C), F32),
        vmem((half_m, C), F32),
        vmem((half_m, C), BF16),
        vmem((half_m, C), BF16),
        vmem((2, half_m, C), F32),
        vmem((2, half_f, C), F32),
        vmem((half_f, C), F32),
        vmem((half_f, C), BF16),
        vmem((half_f, C), BF16),
        vmem((2, half_f, C), F32),
        pltpu.SemaphoreType.DMA((17,)),
        pltpu.SemaphoreType.DMA((qn,)),
        pltpu.SemaphoreType.DMA((qn,)),
        pltpu.SemaphoreType.DMA((qn,)),
        pltpu.SemaphoreType.DMA((qn,)),
        pltpu.SemaphoreType.DMA((zn,)),
        pltpu.SemaphoreType.DMA((zn,)),
        pltpu.SemaphoreType.DMA((zn,)),
        pltpu.SemaphoreType.DMA((zn,)),
        pltpu.SemaphoreType.DMA((zn,)),
        pltpu.SemaphoreType.DMA((zn,)),
        pltpu.SemaphoreType.DMA((qn,)),
        pltpu.SemaphoreType.DMA((qn,)),
        pltpu.SemaphoreType.DMA((4,)),
        pltpu.SemaphoreType.DMA((4,)),
        pltpu.SemaphoreType.DMA((6,)),
        pltpu.SemaphoreType.DMA((6,)),
    ]
    anywhere = pl.BlockSpec(memory_space=pl.ANY)
    shapes = (
        jax.ShapeDtypeStruct((2, CZ, 2, cx), F32),
        jax.ShapeDtypeStruct((2, C), F32),
        jax.ShapeDtypeStruct(velocity.shape, F32),
        jax.ShapeDtypeStruct((9 * CIN, C), F32),
        jax.ShapeDtypeStruct((2, half_m, C), F32),
    )
    results = pl.pallas_call(
        kernel,
        out_shape=shapes,
        in_specs=[anywhere] * 7,
        out_specs=(anywhere,) * 5,
        scratch_shapes=scratch,
        compiler_params=pltpu.CompilerParams(
            collective_id=0, has_side_effects=True, vmem_limit_bytes=60 * 2**20
        ),
    )(
        owner_map.reshape(1, tiles),
        train_order,
        target_stress.transpose(0, 1, 3, 2),
        w_out[0].T,
        velocity,
        w_first[0],
        w_mid[0],
    )
    stress, grad_out, new_velocity, grad_first, grad_mid = pl.pallas_call(
        hand_on,
        out_shape=shapes,
        in_specs=[anywhere] * 5,
        out_specs=(anywhere,) * 5,
        scratch_shapes=[pltpu.VMEM(s.shape, s.dtype) for s in shapes]
        + [pltpu.SemaphoreType.DMA((7,)), pltpu.SemaphoreType.DMA((7,))],
        compiler_params=pltpu.CompilerParams(vmem_limit_bytes=60 * 2**20),
    )(*results)
    return (
        new_velocity,
        stress.transpose(0, 1, 3, 2),
        grad_first[None],
        grad_mid.reshape(1, 9 * C, C),
        grad_out.T[None],
    )


def solution(mesh):
    placed = (
        P(None, "les", None, "cnn"),
        P(None, "les", "cnn", None),
        P(("les", "cnn"), None),
        P(("les", "cnn"), None),
        P("les", None, None),
        P("les", None, None),
        P("les", None, None),
    )
    return jax.shard_map(
        per_device,
        mesh=mesh,
        in_specs=placed,
        out_specs=(
            P(None, "les", None, "cnn"),
            P(None, "les", "cnn", None),
            P("les", None, None),
            P("les", None, None),
            P("les", None, None),
        ),
        check_vma=False,
    )
```

```python
import functools
import math

import jax
import jax.numpy as jnp
from jax import lax
from jax.experimental import pallas as pl
from jax.experimental.pallas import tpu as pltpu
from jax.sharding import PartitionSpec as P

TX = 4
NPL = 16
CZ = 2
NCNN = 4
C = 128
CIN = 48
CAP = 2
DT_STEP = 0.25
VISCOSITY = 0.05
FORCING = 0.2
GHOST = 8
DATA = TX * CZ * CIN
PRED = 128
MESH = pl.DeviceIdType.MESH
F32 = jnp.float32
BF16 = jnp.bfloat16


def z_extent(les_size):
    return 16 if les_size == 128 else 2


def dot(a, b):
    return lax.dot_general(a, b, (((1,), (0,)), ((), ())), preferred_element_type=F32)


def dot_nt(a, b):
    return lax.dot_general(a, b, (((1,), (1,)), ((), ())), preferred_element_type=F32)


def dot_tn(a, b):
    return lax.dot_general(a, b, (((0,), (0,)), ((), ())), preferred_element_type=F32)


def iota(shape, dim):
    return lax.broadcasted_iota(jnp.int32, shape, dim)


def log2(n):
    return n.bit_length() - 1


def gate(values):
    logistic = 0.5 * jnp.tanh(0.5 * values) + 0.5
    return values * logistic, logistic * (1.0 + values * (1.0 - logistic))


def kernel(
    own_hbm, ord_hbm, tgt_hbm, wo_hbm, vel_hbm, wf_hbm, wm_hbm,
    ws_hbm, go_hbm, nv_hbm, gf_hbm, gm_hbm,
    own_ref, ord_ref, tgt_ref, wo_ref, ws_ref, go_ref,
    walls, v, nv, wf, wm, t_one, m_fwd, m_bwd, wo_t, sel, from_owner,
    s1, x1, z0, z1, s1_more, x1_more, z0_more, z1_more, r0, r3, hs, hr, xs, xr,
    h_one, h_one_t, h_two, slope_one, slope_two, g_two, gp_two,
    m_part, m_in, m_send, m_got, m_tot, f_part, f_in, f_send, f_got, f_tot,
    local_sem, q_send, q_recv, qm_send, qm_recv, zs_send, zs_recv, zm_send, zm_recv,
    r_send, r_recv,
    halo_send, halo_recv, grad_send, grad_recv,
):
    les_size = lax.axis_size("les")
    zn = z_extent(les_size)
    qn = les_size // zn
    rows = CAP * les_size
    _, _, ny, cx = vel_hbm.shape
    tiles = 2 * cx // TX
    both = 2 * cx
    loss_scale = 1.0 / math.sqrt(TX * CZ * tiles * NCNN)

    les, cnn = lax.axis_index("les"), lax.axis_index("cnn")
    z, q = les // qn, les % qn
    right, left = (les + 1) % les_size, (les + les_size - 1) % les_size
    east, west, across = (cnn + 1) % NCNN, (cnn + 3) % NCNN, (cnn + 2) % NCNN
    core = cnn % 2
    other = 1 - core
    twin = cnn + 1 - 2 * core

    def q_peer(step):
        return (q + step) % qn

    def z_peer(step):
        return (z + step) % zn

    far_first = sorted(range(1, zn), key=lambda s: -min(s, zn - s))
    turn = zn // 4

    def place(step):
        return (turn - step) % zn

    q_order = list(range(1, qn))

    barrier = pltpu.get_barrier_semaphore()
    greeted = 0
    for step in range(1, qn):
        pl.semaphore_signal(barrier, 1, device_id={"les": z * qn + q_peer(step)}, device_id_type=MESH)
        greeted += 1
    for step in range(1, zn):
        pl.semaphore_signal(barrier, 1, device_id={"les": z_peer(step) * qn + q}, device_id_type=MESH)
        greeted += 1
    for peer in (left, right):
        pl.semaphore_signal(barrier, 1, device_id={"les": peer}, device_id_type=MESH)
        greeted += 1
    for step in range(1, NCNN):
        pl.semaphore_signal(barrier, 1, device_id={"cnn": (cnn + step) % NCNN}, device_id_type=MESH)
        greeted += 1

    low_copy = pltpu.make_async_copy(vel_hbm.at[:, :, pl.ds(0, NPL), :], walls.at[0], local_sem.at[0])
    high_copy = pltpu.make_async_copy(vel_hbm.at[:, :, pl.ds(ny - NPL, NPL), :], walls.at[1], local_sem.at[1])
    v_copy = pltpu.make_async_copy(vel_hbm, v.at[:, :, pl.ds(GHOST, ny), :], local_sem.at[2])
    wf_copy = pltpu.make_async_copy(wf_hbm, wf, local_sem.at[3])
    wm_copy = pltpu.make_async_copy(wm_hbm, wm, local_sem.at[4])
    small_copies = [
        pltpu.make_async_copy(src, dst, local_sem.at[9 + i])
        for i, (src, dst) in enumerate(
            ((own_hbm, own_ref), (ord_hbm, ord_ref), (tgt_hbm, tgt_ref), (wo_hbm, wo_ref))
        )
    ]
    for copy in small_copies + [low_copy, high_copy, v_copy, wf_copy, wm_copy]:
        copy.start()
    for copy in small_copies:
        copy.wait()

    own_row = own_ref[...].astype(F32)
    train_row = jnp.where(ord_ref[...] < tiles // 2, 1.0, 0.0)
    eye = iota((tiles, tiles), 0) == iota((tiles, tiles), 1)
    own_col = jnp.sum(jnp.where(eye, own_row, 0.0), axis=1, keepdims=True)
    train_col = jnp.sum(jnp.where(eye, train_row, 0.0), axis=1, keepdims=True)
    lane_tile = iota((tiles, both), 1) >> log2(TX)
    tile_row = iota((tiles, both), 0)
    hit = lane_tile == tile_row
    own_lane = jnp.sum(jnp.where(hit, own_col, 0.0), axis=0, keepdims=True)
    train_lane = jnp.sum(jnp.where(hit, train_col, 0.0), axis=0, keepdims=True)
    before = jnp.logical_and(own_col == own_lane, tile_row < lane_tile)
    rank_lane = jnp.sum(jnp.where(before, 1.0, 0.0), axis=0, keepdims=True).astype(jnp.int32)
    owner = own_lane.astype(jnp.int32)
    slot = (owner & (qn - 1)) * (CAP * zn) + (owner >> log2(qn)) * CAP + rank_lane
    sel[...] = jnp.where(iota((rows, both), 0) == slot, 1.0, 0.0).astype(BF16)
    owner_row = iota((les_size, both), 0)
    for k in range(CAP):
        mine = jnp.logical_and(owner_row == owner, rank_lane == k)
        from_owner[k] = jnp.where(mine, 1.0, 0.0).astype(BF16)

    low_copy.wait()
    high_copy.wait()
    planes = CZ * 3 * NPL
    order = [(zz, c) for zz in range(CZ) for c in range(3)]
    low = jnp.concatenate([walls[0, c, zz] for zz, c in order], axis=0).astype(BF16)
    high = jnp.concatenate([walls[1, c, zz] for zz, c in order], axis=0).astype(BF16)
    fr, fc = iota((planes, planes), 0), iota((planes, planes), 1)
    group = fr >> log2(NPL)
    turned = jnp.logical_and(group == (fc >> log2(NPL)), (fr & (NPL - 1)) + (fc & (NPL - 1)) == NPL - 1)
    sign = jnp.where(jnp.logical_or(group == 1, group == 4), -1.0, 1.0)
    flip = jnp.where(turned, sign, 0.0).astype(BF16)
    cells = jnp.concatenate([low.astype(F32), dot(flip, high)], axis=1)
    cell_x = iota((planes, both), 1) & (TX - 1)
    pieces = [jnp.where(cell_x == xx, cells, 0.0).astype(BF16) for xx in range(TX)]
    goal = [
        jnp.concatenate([tgt_ref[b, zz].astype(F32) for zz in range(CZ)], axis=0) for b in range(2)
    ]
    goal = jnp.concatenate(goal, axis=1)
    goal = jnp.concatenate([goal] * TX, axis=0)
    small_x = iota((16, both), 1) & (TX - 1)
    small_row = iota((16, both), 0)
    more = [
        jnp.where(small_x == (small_row >> 2), goal, 0.0).astype(BF16),
        jnp.where(small_x == 0, jnp.broadcast_to(train_lane, (16, both)), 0.0).astype(BF16),
        jnp.zeros((PRED - 32, both), BF16),
    ]
    packed = dot_nt(sel[...], jnp.concatenate(pieces, axis=0)).astype(BF16)
    s1[...] = packed.reshape(qn, CAP * zn, DATA)
    packed = dot_nt(sel[...], jnp.concatenate(more, axis=0)).astype(BF16)
    s1_more[...] = packed.reshape(qn, CAP * zn, PRED)

    pl.semaphore_wait(barrier, greeted)

    sends = []

    def spread_q(src, dst, send_sem, recv_sem):
        copies = []
        for step in q_order:
            copy = pltpu.make_async_remote_copy(
                src.at[q_peer(step)], dst.at[q], send_sem.at[step], recv_sem.at[step],
                device_id={"les": z * qn + q_peer(step)}, device_id_type=MESH,
            )
            copy.start()
            copies.append(copy)
        sends.extend(copies)
        dst[q] = src[q]
        return copies

    def spread_z(src, dst, send_sem, recv_sem):
        copies = []
        for step in far_first:
            copy = pltpu.make_async_remote_copy(
                src.at[z_peer(step)], dst.at[place(step)], send_sem.at[step], recv_sem.at[step],
                device_id={"les": z_peer(step) * qn + q}, device_id_type=MESH,
            )
            copy.start()
            copies.append(copy)
        sends.extend(copies)
        dst[place(0)] = src[z]
        return dict(zip(far_first, copies))

    q_copies = spread_q(s1, x1, q_send, q_recv)
    qm_copies = spread_q(s1_more, x1_more, qm_send, qm_recv)

    v_copy.wait()
    for zz in range(CZ):
        hs[zz] = v[:, zz, GHOST : GHOST + ny, :].astype(BF16)
    halo_copies = [
        pltpu.make_async_remote_copy(
            hs.at[1], hr.at[0], halo_send.at[0], halo_recv.at[0], device_id={"les": right}, device_id_type=MESH
        ),
        pltpu.make_async_remote_copy(
            hs.at[0], hr.at[1], halo_send.at[1], halo_recv.at[1], device_id={"les": left}, device_id_type=MESH
        ),
    ]
    yl = xs.shape[2]
    per_column = ny // yl
    er, ec = iota((16, cx), 0), iota((16, cx), 1)
    first_or_last = jnp.logical_or(
        jnp.logical_and(er == 0, ec == 0), jnp.logical_and(er == 1, ec == cx - 1)
    )
    edges = jnp.where(first_or_last, 1.0, 0.0).astype(BF16)
    xs[...] = jnp.zeros(xs.shape, F32)
    for c in range(3):
        for zz in range(CZ):
            column = dot_nt(edges, hs[zz, c])
            for part in range(per_column):
                j = (c * CZ + zz) * per_column + part
                for side in range(2):
                    xs[side, j : j + 1, :] = column[side : side + 1, part * yl : (part + 1) * yl]
    x_copies = [
        pltpu.make_async_remote_copy(
            xs.at[1], xr.at[0], halo_send.at[2], halo_recv.at[2], device_id={"cnn": east}, device_id_type=MESH
        ),
        pltpu.make_async_remote_copy(
            xs.at[0], xr.at[1], halo_send.at[3], halo_recv.at[3], device_id={"cnn": west}, device_id_type=MESH
        ),
    ]

    pr, pc = iota((rows, rows), 0), iota((rows, rows), 1)
    moved = ((pr >> 1) & (qn - 1)) * (CAP * zn) + (pr >> log2(CAP * qn)) * CAP + (pr & 1)
    to_z = jnp.where(pc == moved, 1.0, 0.0).astype(BF16)
    for copy in q_copies:
        copy.wait_recv()
    z0[...] = dot(to_z, x1[...].reshape(rows, DATA)).astype(BF16).reshape(zn, CAP * qn, DATA)
    z_copies = spread_z(z0, z1, zs_send, zs_recv)
    for copy in qm_copies:
        copy.wait_recv()
    z0_more[...] = dot(to_z, x1_more[...].reshape(rows, PRED)).astype(BF16).reshape(zn, CAP * qn, PRED)
    zm_copies = spread_z(z0_more, z1_more, zm_send, zm_recv)
    for copy in halo_copies + x_copies:
        copy.start()
    sends.extend(halo_copies + x_copies)

    wf_copy.wait()
    wm_copy.wait()
    t_one[...] = jnp.zeros(t_one.shape, BF16)
    for xi in range(TX):
        for zi in range(CZ):
            for xo in range(max(0, xi - 1), min(TX, xi + 2)):
                for zo in range(CZ):
                    tap = 3 * (zi - zo + 1) + (xi - xo + 1)
                    at_row, at_lane = (xi * CZ + zi) * CIN, (xo * CZ + zo) * C
                    t_one[at_row : at_row + CIN, at_lane : at_lane + C] = wf[tap * CIN : (tap + 1) * CIN, :]
    wide = CZ * C
    for dx in (-1, 0, 1):
        for zi in range(CZ):
            for zo in range(CZ):
                tap = 3 * (zi - zo + 1) + (dx + 1)
                block = wm[tap * C : (tap + 1) * C, :]
                m_fwd[(dx + 1) * wide + zi * C : (dx + 1) * wide + (zi + 1) * C, zo * C : (zo + 1) * C] = block
                m_bwd[zi * C : (zi + 1) * C, (1 - dx) * wide + zo * C : (1 - dx) * wide + (zo + 1) * C] = block
    out_w = wo_ref[...].astype(F32)
    wr = iota((PRED, C), 0)
    w16 = jnp.where(wr < CAP * 16, wr & 15, PRED)
    for cell in range(TX * CZ):
        block = jnp.where(w16 == 2 * cell, out_w[0:1], jnp.where(w16 == 2 * cell + 1, out_w[1:2], 0.0))
        wo_t[:, cell * C : (cell + 1) * C] = block.astype(BF16)

    def near(x):
        return max(0, x - 1), min(TX, x + 2)

    half = rows // 2
    fold = jnp.where(iota((half // 2, half), 0) == (iota((half // 2, half), 1) >> 1), 1.0, 0.0).astype(BF16)
    own_lanes = (iota((half, PRED), 1) >> 4) == (iota((half, PRED), 0) & 1)
    predicted = []

    def forward(top):
        here = slice(top, top + half)
        data = z1[top // (CAP * qn) : (top + half) // (CAP * qn)].reshape(half, DATA)
        for x in range(TX):
            lanes = slice(x * wide, (x + 1) * wide)
            value, slope = gate(dot(data, t_one[:, lanes]))
            h_one[here, lanes] = value.astype(BF16)
            slope_one[here, lanes] = slope
        for x in range(TX):
            lanes = slice(x * wide, (x + 1) * wide)
            lo, hi = near(x)
            weights = m_fwd[(lo - x + 1) * wide : (hi - x + 1) * wide, :]
            value, slope = gate(dot(h_one[here, lo * wide : hi * wide], weights))
            h_two[here, lanes] = (value + h_one[here, lanes].astype(F32)).astype(BF16)
            slope_two[here, lanes] = slope
        result = dot_nt(h_two[here, :], wo_t[...])
        predicted.append(result)
        folded = dot(fold, jnp.where(own_lanes, result, 0.0).astype(BF16))
        r0[top // 2 : (top + half) // 2] = folded.reshape(half // 2, 1, PRED)

    def send_row(row, peer):
        pltpu.make_async_remote_copy(
            r0.at[row], r3.at[les], r_send, r_recv, device_id={"les": peer}, device_id_type=MESH
        ).start()

    def send_places(first, last):
        def body(p, carry):
            peer_z = (z + p + zn - turn) % zn
            for k in range(qn):
                send_row(p * qn + k, peer_z * qn + k)
            return carry

        lax.fori_loop(first, last, body, 0)

    for step in far_first:
        if place(step) < zn // 2:
            z_copies[step].wait_recv()
    forward(0)
    for step in range(1, qn):
        send_row(turn * qn + q_peer(step), z * qn + q_peer(step))
    r3[les] = r0[turn * qn + q]
    send_places(0, turn)
    send_places(turn + 1, zn // 2)
    for step in far_first:
        if place(step) >= zn // 2:
            z_copies[step].wait_recv()
    forward(half)
    send_places(zn // 2, zn)

    for copy in zm_copies.values():
        copy.wait_recv()
    data = z1[...].reshape(rows, DATA)
    predicted = jnp.concatenate(predicted, axis=0)
    extra = z1_more[...].reshape(rows, PRED).astype(F32)
    miss = jnp.where(iota((rows, PRED), 1) < 16, predicted - extra, 0.0)
    error = ((2.0 * loss_scale) * extra[:, 16:17] * miss).astype(BF16)
    for x in range(TX):
        lanes = slice(x * wide, (x + 1) * wide)
        grad = dot(error, wo_t[:, lanes])
        g_two[:, lanes] = grad
        gp_two[:, lanes] = (grad * slope_two[:, lanes]).astype(BF16)
    h_one_t[...] = h_one[...].T
    half_m = m_part.shape[1]

    def put_m(tap, value):
        start = tap * C
        while value.shape[0]:
            part, at = start // half_m, start % half_m
            take = min(value.shape[0], half_m - at)
            m_part[part, at : at + take, :] = value[:take]
            value, start = value[take:], start + take

    for dx in (-1, 0, 1):
        total = None
        for x in range(TX):
            if 0 <= x + dx < TX:
                term = dot(
                    h_one_t[(x + dx) * wide : (x + dx + 1) * wide, :], gp_two[:, x * wide : (x + 1) * wide]
                )
                total = term if total is None else total + term
        put_m(dx + 1, total[:C, C:])
        put_m(3 + dx + 1, total[:C, :C] + total[C:, C:])
        put_m(6 + dx + 1, total[C:, :C])

    def exchange(src, dst, index, peer):
        copy = pltpu.make_async_remote_copy(
            src, dst, grad_send.at[index], grad_recv.at[index], device_id={"cnn": peer}, device_id_type=MESH
        )
        copy.start()
        sends.append(copy)
        return copy

    m_first = exchange(m_part.at[other], m_in, 0, twin)

    data_t = data.T
    g_first = [None] * 9
    for x in range(TX):
        lanes = slice(x * wide, (x + 1) * wide)
        lo, hi = near(x)
        weights = m_bwd[:, (lo - x + 1) * wide : (hi - x + 1) * wide]
        grad = g_two[:, lanes] + dot_nt(gp_two[:, lo * wide : hi * wide], weights)
        gp_one = (grad * slope_one[:, lanes]).astype(BF16)
        lo_row, hi_row = lo * planes, hi * planes
        product = dot(data_t[lo_row:hi_row], gp_one)
        for xi in range(lo, hi):
            for zi in range(CZ):
                for zo in range(CZ):
                    tap = 3 * (zi - zo + 1) + (xi - x + 1)
                    at_row = (xi - lo) * planes + zi * CIN
                    piece = product[at_row : at_row + CIN, zo * C : (zo + 1) * C]
                    g_first[tap] = piece if g_first[tap] is None else g_first[tap] + piece
    half_f = f_part.shape[1]
    for tap in range(9):
        start, value = tap * CIN, g_first[tap]
        while value.shape[0]:
            part, at = start // half_f, start % half_f
            take = min(value.shape[0], half_f - at)
            f_part[part, at : at + take, :] = value[:take]
            value, start = value[take:], start + take
    cross = dot_tn(error, h_two[...])
    g_out = None
    for cell in range(TX * CZ):
        piece = cross[2 * cell : 2 * cell + 2, cell * C : (cell + 1) * C]
        g_out = piece if g_out is None else g_out + piece
    out_at = 9 * CIN - half_f
    f_part[1, out_at:half_f, :] = jnp.zeros((half_f - out_at, C), F32)
    f_part[1, out_at : out_at + 2, :] = g_out
    f_first = exchange(f_part.at[other], f_in, 1, twin)

    m_first.wait_recv()
    m_send[...] = (m_part[core] + m_in[...]).astype(BF16)
    m_second = exchange(m_send, m_got, 2, across)

    f_first.wait_recv()
    f_send[...] = (f_part[core] + f_in[...]).astype(BF16)
    f_second = exchange(f_send, f_got, 3, across)

    for c in range(3):
        mirror = -1.0 if c == 1 else 1.0
        for zz in range(CZ):
            v[c, zz, GHOST - 1 : GHOST, :] = mirror * v[c, zz, GHOST : GHOST + 1, :]
            v[c, zz, GHOST + ny : GHOST + ny + 1, :] = mirror * v[c, zz, GHOST + ny - 1 : GHOST + ny, :]
    for copy in halo_copies + x_copies:
        copy.wait_recv()
    columns = [xr[side].T for side in range(2)]
    chunk = min(64, yl)
    lane = iota((chunk, cx), 1)
    for zz in range(CZ):
        for start in range(0, ny, chunk):
            here = slice(GHOST + start, GHOST + start + chunk)
            speed = [v[c, zz, here, :] for c in range(3)]
            for c in range(3):
                center = speed[c]
                j = (c * CZ + zz) * per_column + start // yl
                at = start % yl
                x_minus = jnp.where(
                    lane == 0, columns[0][at : at + chunk, j : j + 1], pltpu.roll(center, 1, 1)
                )
                x_plus = jnp.where(
                    lane == cx - 1, columns[1][at : at + chunk, j : j + 1], pltpu.roll(center, cx - 1, 1)
                )
                y_minus = v[c, zz, GHOST + start - 1 : GHOST + start - 1 + chunk, :]
                y_plus = v[c, zz, GHOST + start + 1 : GHOST + start + 1 + chunk, :]
                if zz == 0:
                    z_minus, z_plus = hr[0, c, start : start + chunk, :].astype(F32), v[c, 1, here, :]
                else:
                    z_minus, z_plus = v[c, 0, here, :], hr[1, c, start : start + chunk, :].astype(F32)
                advect = 0.5 * (
                    speed[0] * (x_plus - x_minus)
                    + speed[1] * (y_plus - y_minus)
                    + speed[2] * (z_plus - z_minus)
                )
                laplace = x_plus + x_minus + z_plus + z_minus + y_plus + y_minus - 6.0 * center
                change = VISCOSITY * laplace - advect
                if c == 0:
                    change = change + FORCING
                nv[c, zz, start : start + chunk, :] = center + DT_STEP * change

    rim = 8
    body = pltpu.make_async_copy(
        nv.at[:, :, pl.ds(rim, ny - 2 * rim), :], nv_hbm.at[:, :, pl.ds(rim, ny - 2 * rim), :], local_sem.at[5]
    )
    body.start()

    m_second.wait_recv()
    m_tot[core] = m_send[...].astype(F32) + m_got[...].astype(F32)
    m_third = exchange(m_tot.at[core], m_tot.at[core], 4, twin)

    f_second.wait_recv()
    f_tot[core] = f_send[...].astype(F32) + f_got[...].astype(F32)
    f_third = exchange(f_tot.at[core], f_tot.at[core], 5, twin)

    everyone = pl.ds(0, les_size - 1)
    pltpu.make_async_copy(r0.at[everyone], r3.at[everyone], r_recv).wait()
    back = r3[...].reshape(les_size, PRED).astype(BF16)
    arrived = dot_tn(back, from_owner[0])[:16] + dot_tn(back, from_owner[1])[16:32]
    wide_x = iota((2 * CZ, both), 1) & (TX - 1)
    stress = jnp.zeros((2 * CZ, both), F32)
    for xx in range(TX):
        stress = jnp.where(wide_x == xx, arrived[xx * 2 * CZ : (xx + 1) * 2 * CZ, :], stress)
    for b in range(2):
        row = 0 if b == 0 else ny - 1
        for zz in range(CZ):
            part = stress[zz * 2 : zz * 2 + 2, b * cx : (b + 1) * cx]
            ws_ref[b, zz] = part
            for m in range(2):
                c = 2 * m
                nv[c, zz, row : row + 1, :] = nv[c, zz, row : row + 1, :] - DT_STEP * part[m : m + 1]
    rims = [
        pltpu.make_async_copy(
            nv.at[:, :, pl.ds(at, rim), :], nv_hbm.at[:, :, pl.ds(at, rim), :], local_sem.at[13 + i]
        )
        for i, at in enumerate((0, ny - rim))
    ]
    rims.append(pltpu.make_async_copy(ws_ref, ws_hbm, local_sem.at[15]))
    for copy in rims:
        copy.start()

    m_third.wait_recv()
    gm_copy = pltpu.make_async_copy(m_tot, gm_hbm, local_sem.at[6])
    gm_copy.start()
    f_third.wait_recv()
    gf_low = pltpu.make_async_copy(f_tot.at[0], gf_hbm.at[pl.ds(0, half_f), :], local_sem.at[7])
    gf_high = pltpu.make_async_copy(
        f_tot.at[1, pl.ds(0, out_at), :], gf_hbm.at[pl.ds(half_f, out_at), :], local_sem.at[8]
    )
    gf_low.start()
    gf_high.start()
    go_ref[...] = f_tot[1, out_at : out_at + 2, :]
    go_copy = pltpu.make_async_copy(go_ref, go_hbm, local_sem.at[16])
    go_copy.start()
    for copy in sends:
        copy.wait_send()
    pltpu.make_async_copy(r0.at[everyone], r3.at[everyone], r_send).wait()
    for copy in rims + [body, gm_copy, gf_low, gf_high, go_copy]:
        copy.wait()


def hand_on(*refs):
    count = (len(refs) - 2) // 3
    given, results, held = refs[:count], refs[count : 2 * count], refs[2 * count : 3 * count]
    into, out = refs[-2:]
    parts = [(i, k) for i in range(count) for k in range(given[i].shape[0] if given[i].shape[0] == 3 else 1)]

    def pick(ref, k):
        return ref.at[k] if ref.shape[0] == 3 else ref

    loads = [
        pltpu.make_async_copy(pick(given[i], k), pick(held[i], k), into.at[n]) for n, (i, k) in enumerate(parts)
    ]
    stores = [
        pltpu.make_async_copy(pick(held[i], k), pick(results[i], k), out.at[n]) for n, (i, k) in enumerate(parts)
    ]
    for load in loads:
        load.start()
    for load, store in zip(loads, stores):
        load.wait()
        store.start()
    for store in stores:
        store.wait()


def per_device(velocity, target_stress, owner_map, train_order, w_first, w_mid, w_out):
    les_size = lax.axis_size("les")
    zn = z_extent(les_size)
    qn = les_size // zn
    rows = CAP * les_size
    _, _, ny, cx = velocity.shape
    tiles = owner_map.shape[0]
    hidden = TX * CZ * C
    half_m, half_f = 9 * C // 2, 224
    yl = min(128, ny)
    vmem = pltpu.VMEM
    scratch = [
        vmem((1, tiles), jnp.int32),
        vmem((1, tiles), jnp.int32),
        vmem((2, CZ, 2, cx), BF16),
        vmem((2, C), BF16),
        vmem((2, CZ, 2, cx), F32),
        vmem((2, C), F32),
        vmem((2, 3, CZ, NPL, cx), F32),
        vmem((3, CZ, ny + 2 * GHOST, cx), F32),
        vmem((3, CZ, ny, cx), F32),
        vmem((9 * CIN, C), BF16),
        vmem((9 * C, C), BF16),
        vmem((TX * CZ * CIN, hidden), BF16),
        vmem((3 * CZ * C, CZ * C), BF16),
        vmem((CZ * C, 3 * CZ * C), BF16),
        vmem((PRED, hidden), BF16),
        vmem((rows, 2 * cx), BF16),
        vmem((CAP, les_size, 2 * cx), BF16),
        vmem((qn, CAP * zn, DATA), BF16),
        vmem((qn, CAP * zn, DATA), BF16),
        vmem((zn, CAP * qn, DATA), BF16),
        vmem((zn, CAP * qn, DATA), BF16),
        vmem((qn, CAP * zn, PRED), BF16),
        vmem((qn, CAP * zn, PRED), BF16),
        vmem((zn, CAP * qn, PRED), BF16),
        vmem((zn, CAP * qn, PRED), BF16),
        vmem((les_size, 1, PRED), F32),
        vmem((les_size, 1, PRED), F32),
        vmem((CZ, 3, ny, cx), BF16),
        vmem((CZ, 3, ny, cx), BF16),
        vmem((2, 16, yl), F32),
        vmem((2, 16, yl), F32),
        vmem((rows, hidden), BF16),
        vmem((hidden, rows), BF16),
        vmem((rows, hidden), BF16),
        vmem((rows, hidden), F32),
        vmem((rows, hidden), F32),
        vmem((rows, hidden), F32),
        vmem((rows, hidden), BF16),
        vmem((2, half_m, C), F32),
        vmem((half_m, C), F32),
        vmem((half_m, C), BF16),
        vmem((half_m, C), BF16),
        vmem((2, half_m, C), F32),
        vmem((2, half_f, C), F32),
        vmem((half_f, C), F32),
        vmem((half_f, C), BF16),
        vmem((half_f, C), BF16),
        vmem((2, half_f, C), F32),
        pltpu.SemaphoreType.DMA((17,)),
        pltpu.SemaphoreType.DMA((qn,)),
        pltpu.SemaphoreType.DMA((qn,)),
        pltpu.SemaphoreType.DMA((qn,)),
        pltpu.SemaphoreType.DMA((qn,)),
        pltpu.SemaphoreType.DMA((zn,)),
        pltpu.SemaphoreType.DMA((zn,)),
        pltpu.SemaphoreType.DMA((zn,)),
        pltpu.SemaphoreType.DMA((zn,)),
        pltpu.SemaphoreType.DMA(()),
        pltpu.SemaphoreType.DMA(()),
        pltpu.SemaphoreType.DMA((4,)),
        pltpu.SemaphoreType.DMA((4,)),
        pltpu.SemaphoreType.DMA((6,)),
        pltpu.SemaphoreType.DMA((6,)),
    ]
    anywhere = pl.BlockSpec(memory_space=pl.ANY)
    shapes = (
        jax.ShapeDtypeStruct((2, CZ, 2, cx), F32),
        jax.ShapeDtypeStruct((2, C), F32),
        jax.ShapeDtypeStruct(velocity.shape, F32),
        jax.ShapeDtypeStruct((9 * CIN, C), F32),
        jax.ShapeDtypeStruct((2, half_m, C), F32),
    )
    results = pl.pallas_call(
        kernel,
        out_shape=shapes,
        in_specs=[anywhere] * 7,
        out_specs=(anywhere,) * 5,
        scratch_shapes=scratch,
        compiler_params=pltpu.CompilerParams(
            collective_id=0, has_side_effects=True, vmem_limit_bytes=60 * 2**20
        ),
    )(
        owner_map.reshape(1, tiles),
        train_order,
        target_stress.transpose(0, 1, 3, 2),
        w_out[0].T,
        velocity,
        w_first[0],
        w_mid[0],
    )
    stress, grad_out, new_velocity, grad_first, grad_mid = pl.pallas_call(
        hand_on,
        out_shape=shapes,
        in_specs=[anywhere] * 5,
        out_specs=(anywhere,) * 5,
        scratch_shapes=[pltpu.VMEM(s.shape, s.dtype) for s in shapes]
        + [pltpu.SemaphoreType.DMA((7,)), pltpu.SemaphoreType.DMA((7,))],
        compiler_params=pltpu.CompilerParams(vmem_limit_bytes=60 * 2**20),
    )(*results)
    return (
        new_velocity,
        stress.transpose(0, 1, 3, 2),
        grad_first[None],
        grad_mid.reshape(1, 9 * C, C),
        grad_out.T[None],
    )


def solution(mesh):
    placed = (
        P(None, "les", None, "cnn"),
        P(None, "les", "cnn", None),
        P(("les", "cnn"), None),
        P(("les", "cnn"), None),
        P("les", None, None),
        P("les", None, None),
        P("les", None, None),
    )
    return jax.shard_map(
        per_device,
        mesh=mesh,
        in_specs=placed,
        out_specs=(
            P(None, "les", None, "cnn"),
            P(None, "les", "cnn", None),
            P("les", None, None),
            P("les", None, None),
            P("les", None, None),
        ),
        check_vma=False,
    )
```

```python
import functools
import math

import jax
import jax.numpy as jnp
from jax import lax
from jax.experimental import pallas as pl
from jax.experimental.pallas import tpu as pltpu
from jax.sharding import PartitionSpec as P

TX = 4
NPL = 16
CZ = 2
NCNN = 4
C = 128
CIN = 48
CAP = 2
DT_STEP = 0.25
VISCOSITY = 0.05
FORCING = 0.2
GHOST = 8
DATA = TX * CZ * CIN
PRED = 128
MORE = 32
MESH = pl.DeviceIdType.MESH
F32 = jnp.float32
BF16 = jnp.bfloat16


def z_extent(les_size):
    return 16 if les_size == 128 else 2


def dot(a, b):
    return lax.dot_general(a, b, (((1,), (0,)), ((), ())), preferred_element_type=F32)


def dot_nt(a, b):
    return lax.dot_general(a, b, (((1,), (1,)), ((), ())), preferred_element_type=F32)


def dot_tn(a, b):
    return lax.dot_general(a, b, (((0,), (0,)), ((), ())), preferred_element_type=F32)


def iota(shape, dim):
    return lax.broadcasted_iota(jnp.int32, shape, dim)


def log2(n):
    return n.bit_length() - 1


def gate(values):
    logistic = 0.5 * jnp.tanh(0.5 * values) + 0.5
    return values * logistic, logistic * (1.0 + values * (1.0 - logistic))


def kernel(
    own_hbm, ord_hbm, tgt_hbm, wo_hbm, vel_hbm, wf_hbm, wm_hbm,
    ws_hbm, go_hbm, nv_hbm, gf_hbm, gm_hbm,
    own_ref, ord_ref, tgt_ref, wo_ref, ws_ref, go_ref,
    walls, v, nv, wf, wm, t_one, m_fwd, m_bwd, wo_t, sel, from_owner,
    s1, x1, z0, z1, s1_more, x1_more, z0_more, z1_more, r0, r3, hs, hr, xs, xr,
    h_one, h_one_t, h_two, slope_one, slope_two, g_two, gp_two,
    m_part, m_in, m_send, m_got, m_tot, f_part, f_in, f_send, f_got, f_tot,
    local_sem, q_send, q_recv, qm_send, qm_recv, zs_send, zs_recv, zm_send, zm_recv,
    r_send, r_recv,
    halo_send, halo_recv, grad_send, grad_recv,
):
    les_size = lax.axis_size("les")
    zn = z_extent(les_size)
    qn = les_size // zn
    rows = CAP * les_size
    _, _, ny, cx = vel_hbm.shape
    tiles = 2 * cx // TX
    both = 2 * cx
    loss_scale = 1.0 / math.sqrt(TX * CZ * tiles * NCNN)

    les, cnn = lax.axis_index("les"), lax.axis_index("cnn")
    z, q = les // qn, les % qn
    right, left = (les + 1) % les_size, (les + les_size - 1) % les_size
    east, west, across = (cnn + 1) % NCNN, (cnn + 3) % NCNN, (cnn + 2) % NCNN
    core = cnn % 2
    other = 1 - core
    twin = cnn + 1 - 2 * core

    def q_peer(step):
        return (q + step) % qn

    def z_peer(step):
        return (z + step) % zn

    far_first = sorted(range(1, zn), key=lambda s: -min(s, zn - s))
    turn = zn // 4

    def place(step):
        return (turn - step) % zn

    q_order = list(range(1, qn))

    barrier = pltpu.get_barrier_semaphore()
    greeted = 0
    for step in far_first:
        pl.semaphore_signal(barrier, 1, device_id={"les": z_peer(step) * qn + q}, device_id_type=MESH)
        greeted += 1
    for step in range(1, qn):
        pl.semaphore_signal(barrier, 1, device_id={"les": z * qn + q_peer(step)}, device_id_type=MESH)
        greeted += 1
    for peer in (left, right):
        pl.semaphore_signal(barrier, 1, device_id={"les": peer}, device_id_type=MESH)
        greeted += 1
    for step in range(1, NCNN):
        pl.semaphore_signal(barrier, 1, device_id={"cnn": (cnn + step) % NCNN}, device_id_type=MESH)
        greeted += 1

    low_copy = pltpu.make_async_copy(vel_hbm.at[:, :, pl.ds(0, NPL), :], walls.at[0], local_sem.at[0])
    high_copy = pltpu.make_async_copy(vel_hbm.at[:, :, pl.ds(ny - NPL, NPL), :], walls.at[1], local_sem.at[1])
    v_copy = pltpu.make_async_copy(vel_hbm, v.at[:, :, pl.ds(GHOST, ny), :], local_sem.at[2])
    wf_copy = pltpu.make_async_copy(wf_hbm, wf, local_sem.at[3])
    wm_copy = pltpu.make_async_copy(wm_hbm, wm, local_sem.at[4])
    small_copies = [
        pltpu.make_async_copy(src, dst, local_sem.at[9 + i])
        for i, (src, dst) in enumerate(
            ((own_hbm, own_ref), (ord_hbm, ord_ref), (tgt_hbm, tgt_ref), (wo_hbm, wo_ref))
        )
    ]
    for copy in small_copies + [low_copy, high_copy, v_copy, wf_copy, wm_copy]:
        copy.start()
    for copy in small_copies:
        copy.wait()

    own_row = own_ref[...].astype(F32)
    train_row = jnp.where(ord_ref[...] < tiles // 2, 1.0, 0.0)
    eye = iota((tiles, tiles), 0) == iota((tiles, tiles), 1)
    own_col = jnp.sum(jnp.where(eye, own_row, 0.0), axis=1, keepdims=True)
    train_col = jnp.sum(jnp.where(eye, train_row, 0.0), axis=1, keepdims=True)
    lane_tile = iota((tiles, both), 1) >> log2(TX)
    tile_row = iota((tiles, both), 0)
    hit = lane_tile == tile_row
    own_lane = jnp.sum(jnp.where(hit, own_col, 0.0), axis=0, keepdims=True)
    train_lane = jnp.sum(jnp.where(hit, train_col, 0.0), axis=0, keepdims=True)
    before = jnp.logical_and(own_col == own_lane, tile_row < lane_tile)
    rank_lane = jnp.sum(jnp.where(before, 1.0, 0.0), axis=0, keepdims=True).astype(jnp.int32)
    owner = own_lane.astype(jnp.int32)
    slot = (owner & (qn - 1)) * (CAP * zn) + (owner >> log2(qn)) * CAP + rank_lane
    sel[...] = jnp.where(iota((rows, both), 0) == slot, 1.0, 0.0).astype(BF16)
    owner_row = iota((les_size, both), 0)
    for k in range(CAP):
        mine = jnp.logical_and(owner_row == owner, rank_lane == k)
        from_owner[k] = jnp.where(mine, 1.0, 0.0).astype(BF16)

    low_copy.wait()
    high_copy.wait()
    planes = CZ * 3 * NPL
    order = [(zz, c) for zz in range(CZ) for c in range(3)]
    low = jnp.concatenate([walls[0, c, zz] for zz, c in order], axis=0).astype(BF16)
    high = jnp.concatenate([walls[1, c, zz] for zz, c in order], axis=0).astype(BF16)
    fr, fc = iota((planes, planes), 0), iota((planes, planes), 1)
    group = fr >> log2(NPL)
    turned = jnp.logical_and(group == (fc >> log2(NPL)), (fr & (NPL - 1)) + (fc & (NPL - 1)) == NPL - 1)
    sign = jnp.where(jnp.logical_or(group == 1, group == 4), -1.0, 1.0)
    flip = jnp.where(turned, sign, 0.0).astype(BF16)
    cells = jnp.concatenate([low.astype(F32), dot(flip, high)], axis=1)
    cell_x = iota((planes, both), 1) & (TX - 1)
    pieces = [jnp.where(cell_x == xx, cells, 0.0).astype(BF16) for xx in range(TX)]
    goal = [
        jnp.concatenate([tgt_ref[b, zz].astype(F32) for zz in range(CZ)], axis=0) for b in range(2)
    ]
    goal = jnp.concatenate(goal, axis=1)
    goal = jnp.concatenate([goal] * TX, axis=0)
    small_x = iota((16, both), 1) & (TX - 1)
    small_row = iota((16, both), 0)
    more = [
        jnp.where(small_x == (small_row >> 2), goal, 0.0).astype(BF16),
        jnp.where(small_x == 0, jnp.broadcast_to(train_lane, (16, both)), 0.0).astype(BF16),
    ]
    packed = dot_nt(sel[...], jnp.concatenate(pieces, axis=0)).astype(BF16)
    s1[...] = packed.reshape(qn, CAP * zn, DATA)
    packed = dot_nt(sel[...], jnp.concatenate(more, axis=0)).astype(BF16)
    s1_more[...] = packed.reshape(qn, CAP * zn, MORE)

    pl.semaphore_wait(barrier, greeted)

    sends = []

    def spread_q(src, dst, send_sem, recv_sem):
        copies = []
        for step in q_order:
            copy = pltpu.make_async_remote_copy(
                src.at[q_peer(step)], dst.at[q], send_sem.at[step], recv_sem.at[step],
                device_id={"les": z * qn + q_peer(step)}, device_id_type=MESH,
            )
            copy.start()
            copies.append(copy)
        sends.extend(copies)
        dst[q] = src[q]
        return copies

    def spread_z(src, dst, send_sem, recv_sem):
        copies = []
        for step in far_first:
            copy = pltpu.make_async_remote_copy(
                src.at[z_peer(step)], dst.at[place(step)], send_sem.at[step], recv_sem.at[step],
                device_id={"les": z_peer(step) * qn + q}, device_id_type=MESH,
            )
            copy.start()
            copies.append(copy)
        sends.extend(copies)
        dst[place(0)] = src[z]
        return dict(zip(far_first, copies))

    q_copies = spread_q(s1, x1, q_send, q_recv)
    qm_copies = spread_q(s1_more, x1_more, qm_send, qm_recv)

    v_copy.wait()
    for zz in range(CZ):
        hs[zz] = v[:, zz, GHOST : GHOST + ny, :].astype(BF16)
    halo_copies = [
        pltpu.make_async_remote_copy(
            hs.at[1], hr.at[0], halo_send.at[0], halo_recv.at[0], device_id={"les": right}, device_id_type=MESH
        ),
        pltpu.make_async_remote_copy(
            hs.at[0], hr.at[1], halo_send.at[1], halo_recv.at[1], device_id={"les": left}, device_id_type=MESH
        ),
    ]
    yl = xs.shape[2]
    per_column = ny // yl
    er, ec = iota((16, cx), 0), iota((16, cx), 1)
    first_or_last = jnp.logical_or(
        jnp.logical_and(er == 0, ec == 0), jnp.logical_and(er == 1, ec == cx - 1)
    )
    edges = jnp.where(first_or_last, 1.0, 0.0).astype(BF16)
    xs[...] = jnp.zeros(xs.shape, F32)
    for c in range(3):
        for zz in range(CZ):
            column = dot_nt(edges, hs[zz, c])
            for part in range(per_column):
                j = (c * CZ + zz) * per_column + part
                for side in range(2):
                    xs[side, j : j + 1, :] = column[side : side + 1, part * yl : (part + 1) * yl]
    x_copies = [
        pltpu.make_async_remote_copy(
            xs.at[1], xr.at[0], halo_send.at[2], halo_recv.at[2], device_id={"cnn": east}, device_id_type=MESH
        ),
        pltpu.make_async_remote_copy(
            xs.at[0], xr.at[1], halo_send.at[3], halo_recv.at[3], device_id={"cnn": west}, device_id_type=MESH
        ),
    ]

    pr, pc = iota((rows, rows), 0), iota((rows, rows), 1)
    moved = ((pr >> 1) & (qn - 1)) * (CAP * zn) + (pr >> log2(CAP * qn)) * CAP + (pr & 1)
    to_z = jnp.where(pc == moved, 1.0, 0.0).astype(BF16)
    for copy in q_copies:
        copy.wait_recv()
    z0[...] = dot(to_z, x1[...].reshape(rows, DATA)).astype(BF16).reshape(zn, CAP * qn, DATA)
    z_copies = spread_z(z0, z1, zs_send, zs_recv)
    for copy in qm_copies:
        copy.wait_recv()
    z0_more[...] = dot(to_z, x1_more[...].reshape(rows, MORE)).astype(BF16).reshape(zn, CAP * qn, MORE)
    zm_copies = spread_z(z0_more, z1_more, zm_send, zm_recv)
    for copy in halo_copies + x_copies:
        copy.start()
    sends.extend(halo_copies + x_copies)

    wf_copy.wait()
    wm_copy.wait()
    t_one[...] = jnp.zeros(t_one.shape, BF16)
    for xi in range(TX):
        for zi in range(CZ):
            for xo in range(max(0, xi - 1), min(TX, xi + 2)):
                for zo in range(CZ):
                    tap = 3 * (zi - zo + 1) + (xi - xo + 1)
                    at_row, at_lane = (xi * CZ + zi) * CIN, (xo * CZ + zo) * C
                    t_one[at_row : at_row + CIN, at_lane : at_lane + C] = wf[tap * CIN : (tap + 1) * CIN, :]
    wide = CZ * C
    for dx in (-1, 0, 1):
        for zi in range(CZ):
            for zo in range(CZ):
                tap = 3 * (zi - zo + 1) + (dx + 1)
                block = wm[tap * C : (tap + 1) * C, :]
                m_fwd[(dx + 1) * wide + zi * C : (dx + 1) * wide + (zi + 1) * C, zo * C : (zo + 1) * C] = block
                m_bwd[zi * C : (zi + 1) * C, (1 - dx) * wide + zo * C : (1 - dx) * wide + (zo + 1) * C] = block
    out_w = wo_ref[...].astype(F32)
    wr = iota((PRED, C), 0)
    w16 = jnp.where(wr < CAP * 16, wr & 15, PRED)
    for cell in range(TX * CZ):
        block = jnp.where(w16 == 2 * cell, out_w[0:1], jnp.where(w16 == 2 * cell + 1, out_w[1:2], 0.0))
        wo_t[:, cell * C : (cell + 1) * C] = block.astype(BF16)

    def near(x):
        return max(0, x - 1), min(TX, x + 2)

    half = rows // 2
    fold = jnp.where(iota((half // 2, half), 0) == (iota((half // 2, half), 1) >> 1), 1.0, 0.0).astype(BF16)
    own_lanes = (iota((half, PRED), 1) >> 4) == (iota((half, PRED), 0) & 1)
    predicted = []

    def forward(top):
        here = slice(top, top + half)
        data = z1[top // (CAP * qn) : (top + half) // (CAP * qn)].reshape(half, DATA)
        for x in range(TX):
            lanes = slice(x * wide, (x + 1) * wide)
            value, slope = gate(dot(data, t_one[:, lanes]))
            h_one[here, lanes] = value.astype(BF16)
            slope_one[here, lanes] = slope
        for x in range(TX):
            lanes = slice(x * wide, (x + 1) * wide)
            lo, hi = near(x)
            weights = m_fwd[(lo - x + 1) * wide : (hi - x + 1) * wide, :]
            value, slope = gate(dot(h_one[here, lo * wide : hi * wide], weights))
            h_two[here, lanes] = (value + h_one[here, lanes].astype(F32)).astype(BF16)
            slope_two[here, lanes] = slope
        result = dot_nt(h_two[here, :], wo_t[...])
        predicted.append(result)
        folded = dot(fold, jnp.where(own_lanes, result, 0.0).astype(BF16))
        r0[top // 2 : (top + half) // 2] = folded.reshape(half // 2, 1, PRED)

    def send_row(row, peer):
        pltpu.make_async_remote_copy(
            r0.at[row], r3.at[les], r_send, r_recv, device_id={"les": peer}, device_id_type=MESH
        ).start()

    def send_places(first, last):
        def body(p, carry):
            peer_z = (z + p + zn - turn) % zn
            for k in range(qn):
                send_row(p * qn + k, peer_z * qn + k)
            return carry

        lax.fori_loop(first, last, body, 0)

    for step in far_first:
        if place(step) < zn // 2:
            z_copies[step].wait_recv()
    forward(0)
    h_one_t[:, :half] = h_one[:half, :].T
    for step in far_first:
        if place(step) >= zn // 2:
            z_copies[step].wait_recv()
    forward(half)
    send_places(zn // 2 + turn, zn)
    send_places(zn // 2, zn // 2 + turn)

    for copy in zm_copies.values():
        copy.wait_recv()
    data = z1[...].reshape(rows, DATA)
    predicted = jnp.concatenate(predicted, axis=0)
    extra = z1_more[...].reshape(rows, MORE).astype(F32)
    miss = predicted[:, :16] - extra[:, :16]
    error = ((2.0 * loss_scale) * extra[:, 16:17] * miss).astype(BF16)
    for x in range(TX):
        lanes = slice(x * wide, (x + 1) * wide)
        grad = dot(error, wo_t[:16, lanes])
        g_two[:, lanes] = grad
        gp_two[:, lanes] = (grad * slope_two[:, lanes]).astype(BF16)
    h_one_t[:, half:] = h_one[half:, :].T

    def exchange(src, dst, index, peer):
        copy = pltpu.make_async_remote_copy(
            src, dst, grad_send.at[index], grad_recv.at[index], device_id={"cnn": peer}, device_id_type=MESH
        )
        copy.start()
        sends.append(copy)
        return copy

    share = m_in.shape[1]
    own_part = pl.ds(pl.multiple_of(core * share, share), share)
    twin_part = pl.ds(pl.multiple_of(other * share, share), share)
    m_first = []
    for d, dx in enumerate((-1, 0, 1)):
        total = None
        for x in range(TX):
            if 0 <= x + dx < TX:
                term = dot(
                    h_one_t[(x + dx) * wide : (x + dx + 1) * wide, :], gp_two[:, x * wide : (x + 1) * wide]
                )
                total = term if total is None else total + term
        m_part[d, :C, :] = total[:C, C:]
        m_part[d, C : 2 * C, :] = total[:C, :C] + total[C:, C:]
        m_part[d, 2 * C :, :] = total[C:, :C]
        m_first.append(exchange(m_part.at[d, twin_part], m_in.at[d], d, twin))

    def m_across(d):
        m_first[d].wait_recv()
        m_send[d] = (m_part[d, own_part, :] + m_in[d]).astype(BF16)
        return exchange(m_send.at[d], m_got.at[d], 3 + d, across)

    def m_back(d):
        m_second[d].wait_recv()
        m_tot[d, own_part, :] = m_send[d].astype(F32) + m_got[d].astype(F32)
        return exchange(m_tot.at[d, own_part], m_tot.at[d, own_part], 6 + d, twin)

    send_places(0, turn)
    send_places(turn + 1, zn // 2)
    for step in range(1, qn):
        send_row(turn * qn + q_peer(step), z * qn + q_peer(step))
    r3[les] = r0[turn * qn + q]
    m_second = [m_across(0), m_across(1)]

    data_t = data.T
    g_first = [None] * 9
    for x in range(TX):
        lanes = slice(x * wide, (x + 1) * wide)
        lo, hi = near(x)
        weights = m_bwd[:, (lo - x + 1) * wide : (hi - x + 1) * wide]
        grad = g_two[:, lanes] + dot_nt(gp_two[:, lo * wide : hi * wide], weights)
        if x == 1:
            m_second.append(m_across(2))
        gp_one = (grad * slope_one[:, lanes]).astype(BF16)
        lo_row, hi_row = lo * planes, hi * planes
        product = dot(data_t[lo_row:hi_row], gp_one)
        for xi in range(lo, hi):
            for zi in range(CZ):
                for zo in range(CZ):
                    tap = 3 * (zi - zo + 1) + (xi - x + 1)
                    at_row = (xi - lo) * planes + zi * CIN
                    piece = product[at_row : at_row + CIN, zo * C : (zo + 1) * C]
                    g_first[tap] = piece if g_first[tap] is None else g_first[tap] + piece
    half_f = f_part.shape[1]
    for tap in range(9):
        start, value = tap * CIN, g_first[tap]
        while value.shape[0]:
            part, at = start // half_f, start % half_f
            take = min(value.shape[0], half_f - at)
            f_part[part, at : at + take, :] = value[:take]
            value, start = value[take:], start + take
    cross = dot_tn(error, h_two[...])
    g_out = None
    for cell in range(TX * CZ):
        piece = cross[2 * cell : 2 * cell + 2, cell * C : (cell + 1) * C]
        g_out = piece if g_out is None else g_out + piece
    out_at = 9 * CIN - half_f
    f_part[1, out_at:half_f, :] = jnp.zeros((half_f - out_at, C), F32)
    f_part[1, out_at : out_at + 2, :] = g_out
    f_first = exchange(f_part.at[other], f_in, 9, twin)

    m_third = [m_back(0)]

    f_first.wait_recv()
    f_send[...] = (f_part[core] + f_in[...]).astype(BF16)
    f_second = exchange(f_send, f_got, 10, across)
    m_third.append(m_back(1))

    m_third.append(m_back(2))

    for c in range(3):
        mirror = -1.0 if c == 1 else 1.0
        for zz in range(CZ):
            v[c, zz, GHOST - 1 : GHOST, :] = mirror * v[c, zz, GHOST : GHOST + 1, :]
            v[c, zz, GHOST + ny : GHOST + ny + 1, :] = mirror * v[c, zz, GHOST + ny - 1 : GHOST + ny, :]
    for copy in halo_copies + x_copies:
        copy.wait_recv()
    columns = [xr[side].T for side in range(2)]
    chunk = min(64, yl)
    lane = iota((chunk, cx), 1)
    for zz in range(CZ):
        for start in range(0, ny, chunk):
            here = slice(GHOST + start, GHOST + start + chunk)
            speed = [v[c, zz, here, :] for c in range(3)]
            for c in range(3):
                center = speed[c]
                j = (c * CZ + zz) * per_column + start // yl
                at = start % yl
                x_minus = jnp.where(
                    lane == 0, columns[0][at : at + chunk, j : j + 1], pltpu.roll(center, 1, 1)
                )
                x_plus = jnp.where(
                    lane == cx - 1, columns[1][at : at + chunk, j : j + 1], pltpu.roll(center, cx - 1, 1)
                )
                y_minus = v[c, zz, GHOST + start - 1 : GHOST + start - 1 + chunk, :]
                y_plus = v[c, zz, GHOST + start + 1 : GHOST + start + 1 + chunk, :]
                if zz == 0:
                    z_minus, z_plus = hr[0, c, start : start + chunk, :].astype(F32), v[c, 1, here, :]
                else:
                    z_minus, z_plus = v[c, 0, here, :], hr[1, c, start : start + chunk, :].astype(F32)
                advect = 0.5 * (
                    speed[0] * (x_plus - x_minus)
                    + speed[1] * (y_plus - y_minus)
                    + speed[2] * (z_plus - z_minus)
                )
                laplace = x_plus + x_minus + z_plus + z_minus + y_plus + y_minus - 6.0 * center
                change = VISCOSITY * laplace - advect
                if c == 0:
                    change = change + FORCING
                nv[c, zz, start : start + chunk, :] = center + DT_STEP * change

    rim = 8
    body = pltpu.make_async_copy(
        nv.at[:, :, pl.ds(rim, ny - 2 * rim), :], nv_hbm.at[:, :, pl.ds(rim, ny - 2 * rim), :], local_sem.at[5]
    )
    body.start()

    f_second.wait_recv()
    f_tot[core] = f_send[...].astype(F32) + f_got[...].astype(F32)
    f_third = exchange(f_tot.at[core], f_tot.at[core], 11, twin)

    everyone = pl.ds(0, les_size - 1)
    pltpu.make_async_copy(r0.at[everyone], r3.at[everyone], r_recv).wait()
    back = r3[...].reshape(les_size, PRED).astype(BF16)
    arrived = dot_tn(back, from_owner[0])[:16] + dot_tn(back, from_owner[1])[16:32]
    wide_x = iota((2 * CZ, both), 1) & (TX - 1)
    stress = jnp.zeros((2 * CZ, both), F32)
    for xx in range(TX):
        stress = jnp.where(wide_x == xx, arrived[xx * 2 * CZ : (xx + 1) * 2 * CZ, :], stress)
    for b in range(2):
        row = 0 if b == 0 else ny - 1
        for zz in range(CZ):
            part = stress[zz * 2 : zz * 2 + 2, b * cx : (b + 1) * cx]
            ws_ref[b, zz] = part
            for m in range(2):
                c = 2 * m
                nv[c, zz, row : row + 1, :] = nv[c, zz, row : row + 1, :] - DT_STEP * part[m : m + 1]
    rims = [
        pltpu.make_async_copy(
            nv.at[:, :, pl.ds(at, rim), :], nv_hbm.at[:, :, pl.ds(at, rim), :], local_sem.at[13 + i]
        )
        for i, at in enumerate((0, ny - rim))
    ]
    rims.append(pltpu.make_async_copy(ws_ref, ws_hbm, local_sem.at[15]))
    for copy in rims:
        copy.start()

    for copy in m_third:
        copy.wait_recv()
    gm_copy = pltpu.make_async_copy(m_tot, gm_hbm, local_sem.at[6])
    gm_copy.start()
    f_third.wait_recv()
    gf_low = pltpu.make_async_copy(f_tot.at[0], gf_hbm.at[pl.ds(0, half_f), :], local_sem.at[7])
    gf_high = pltpu.make_async_copy(
        f_tot.at[1, pl.ds(0, out_at), :], gf_hbm.at[pl.ds(half_f, out_at), :], local_sem.at[8]
    )
    gf_low.start()
    gf_high.start()
    go_ref[...] = f_tot[1, out_at : out_at + 2, :]
    go_copy = pltpu.make_async_copy(go_ref, go_hbm, local_sem.at[16])
    go_copy.start()
    for copy in sends:
        copy.wait_send()
    pltpu.make_async_copy(r0.at[everyone], r3.at[everyone], r_send).wait()
    for copy in rims + [body, gm_copy, gf_low, gf_high, go_copy]:
        copy.wait()


def hand_on(ws, go, nv, gf, gm, ws_out, go_out, nv_out, gf_out, gm_out, ws_v, go_v, nv_v, gf_v, gm_v, into, out):
    moves = [((nv.at[c], nv_v.at[c]), [(nv_v.at[c], nv_out.at[c])]) for c in range(3)]
    for d in range(3):
        taps = [
            (gm_v.at[d, pl.ds(k * C, C)], gm_out.at[pl.ds((3 * k + d) * C, C)]) for k in range(3)
        ]
        moves.append(((gm.at[d], gm_v.at[d]), taps))
    moves += [((gf, gf_v), [(gf_v, gf_out)]), ((ws, ws_v), [(ws_v, ws_out)]), ((go, go_v), [(go_v, go_out)])]
    loads = [pltpu.make_async_copy(*load, into.at[n]) for n, (load, _) in enumerate(moves)]
    for load in loads:
        load.start()
    stores = []
    for load, (_, parts) in zip(loads, moves):
        load.wait()
        for part in parts:
            store = pltpu.make_async_copy(*part, out.at[len(stores)])
            store.start()
            stores.append(store)
    for store in stores:
        store.wait()


def per_device(velocity, target_stress, owner_map, train_order, w_first, w_mid, w_out):
    les_size = lax.axis_size("les")
    zn = z_extent(les_size)
    qn = les_size // zn
    rows = CAP * les_size
    _, _, ny, cx = velocity.shape
    tiles = owner_map.shape[0]
    hidden = TX * CZ * C
    share, half_f = 3 * C // 2, 224
    yl = min(128, ny)
    vmem = pltpu.VMEM
    scratch = [
        vmem((1, tiles), jnp.int32),
        vmem((1, tiles), jnp.int32),
        vmem((2, CZ, 2, cx), BF16),
        vmem((2, C), BF16),
        vmem((2, CZ, 2, cx), F32),
        vmem((2, C), F32),
        vmem((2, 3, CZ, NPL, cx), F32),
        vmem((3, CZ, ny + 2 * GHOST, cx), F32),
        vmem((3, CZ, ny, cx), F32),
        vmem((9 * CIN, C), BF16),
        vmem((9 * C, C), BF16),
        vmem((TX * CZ * CIN, hidden), BF16),
        vmem((3 * CZ * C, CZ * C), BF16),
        vmem((CZ * C, 3 * CZ * C), BF16),
        vmem((PRED, hidden), BF16),
        vmem((rows, 2 * cx), BF16),
        vmem((CAP, les_size, 2 * cx), BF16),
        vmem((qn, CAP * zn, DATA), BF16),
        vmem((qn, CAP * zn, DATA), BF16),
        vmem((zn, CAP * qn, DATA), BF16),
        vmem((zn, CAP * qn, DATA), BF16),
        vmem((qn, CAP * zn, MORE), BF16),
        vmem((qn, CAP * zn, MORE), BF16),
        vmem((zn, CAP * qn, MORE), BF16),
        vmem((zn, CAP * qn, MORE), BF16),
        vmem((les_size, 1, PRED), F32),
        vmem((les_size, 1, PRED), F32),
        vmem((CZ, 3, ny, cx), BF16),
        vmem((CZ, 3, ny, cx), BF16),
        vmem((2, 16, yl), F32),
        vmem((2, 16, yl), F32),
        vmem((rows, hidden), BF16),
        vmem((hidden, rows), BF16),
        vmem((rows, hidden), BF16),
        vmem((rows, hidden), F32),
        vmem((rows, hidden), F32),
        vmem((rows, hidden), F32),
        vmem((rows, hidden), BF16),
        vmem((3, 2 * share, C), F32),
        vmem((3, share, C), F32),
        vmem((3, share, C), BF16),
        vmem((3, share, C), BF16),
        vmem((3, 2 * share, C), F32),
        vmem((2, half_f, C), F32),
        vmem((half_f, C), F32),
        vmem((half_f, C), BF16),
        vmem((half_f, C), BF16),
        vmem((2, half_f, C), F32),
        pltpu.SemaphoreType.DMA((17,)),
        pltpu.SemaphoreType.DMA((qn,)),
        pltpu.SemaphoreType.DMA((qn,)),
        pltpu.SemaphoreType.DMA((qn,)),
        pltpu.SemaphoreType.DMA((qn,)),
        pltpu.SemaphoreType.DMA((zn,)),
        pltpu.SemaphoreType.DMA((zn,)),
        pltpu.SemaphoreType.DMA((zn,)),
        pltpu.SemaphoreType.DMA((zn,)),
        pltpu.SemaphoreType.DMA(()),
        pltpu.SemaphoreType.DMA(()),
        pltpu.SemaphoreType.DMA((4,)),
        pltpu.SemaphoreType.DMA((4,)),
        pltpu.SemaphoreType.DMA((12,)),
        pltpu.SemaphoreType.DMA((12,)),
    ]
    anywhere = pl.BlockSpec(memory_space=pl.ANY)
    shapes = (
        jax.ShapeDtypeStruct((2, CZ, 2, cx), F32),
        jax.ShapeDtypeStruct((2, C), F32),
        jax.ShapeDtypeStruct(velocity.shape, F32),
        jax.ShapeDtypeStruct((9 * CIN, C), F32),
        jax.ShapeDtypeStruct((3, 3 * C, C), F32),
    )
    results = pl.pallas_call(
        kernel,
        out_shape=shapes,
        in_specs=[anywhere] * 7,
        out_specs=(anywhere,) * 5,
        scratch_shapes=scratch,
        compiler_params=pltpu.CompilerParams(
            collective_id=0, has_side_effects=True, vmem_limit_bytes=60 * 2**20
        ),
    )(
        owner_map.reshape(1, tiles),
        train_order,
        target_stress.transpose(0, 1, 3, 2),
        w_out[0].T,
        velocity,
        w_first[0],
        w_mid[0],
    )
    stress, grad_out, new_velocity, grad_first, grad_mid = pl.pallas_call(
        hand_on,
        out_shape=shapes[:4] + (jax.ShapeDtypeStruct((9 * C, C), F32),),
        in_specs=[anywhere] * 5,
        out_specs=(anywhere,) * 5,
        scratch_shapes=[pltpu.VMEM(s.shape, s.dtype) for s in shapes]
        + [pltpu.SemaphoreType.DMA((9,)), pltpu.SemaphoreType.DMA((15,))],
        compiler_params=pltpu.CompilerParams(vmem_limit_bytes=60 * 2**20),
    )(*results)
    return (
        new_velocity,
        stress.transpose(0, 1, 3, 2),
        grad_first[None],
        grad_mid[None],
        grad_out.T[None],
    )


def solution(mesh):
    placed = (
        P(None, "les", None, "cnn"),
        P(None, "les", "cnn", None),
        P(("les", "cnn"), None),
        P(("les", "cnn"), None),
        P("les", None, None),
        P("les", None, None),
        P("les", None, None),
    )
    return jax.shard_map(
        per_device,
        mesh=mesh,
        in_specs=placed,
        out_specs=(
            P(None, "les", None, "cnn"),
            P(None, "les", "cnn", None),
            P("les", None, None),
            P("les", None, None),
            P("les", None, None),
        ),
        check_vma=False,
    )
```
